32 devices in a mesh: rep: 2 (over x), dp: 8 (over z, y), tensor: 2 (over core).
Axes of the slice: x: 2, y: 2, z: 4, core: 2. Of those that a mesh axis runs over, the one named last changes fastest.
Arguments:
- rubric_query: bfloat16 [64, 256, 4096], P(('rep', 'dp'), None, 'tensor'), parts along dimension 0, may hold values from -48 to 48
- rubric_key: bfloat16 [64, 256, 512], P(('rep', 'dp'), None, 'tensor'), parts along dimension 0, may hold values from -4 to 4
- rubric_value: bfloat16 [64, 256, 512], P(('rep', 'dp'), None, 'tensor'), parts along dimension 0, may hold values from -6 to 6
- response_states: bfloat16 [64, 256, 8192], P(('rep', 'dp'), None, 'tensor'), parts along dimension 0, may hold values from -6 to 6
- key_weight: bfloat16 [8192, 512], P('tensor'), may hold values from -0.0625 to 0.0625
- value_weight: bfloat16 [8192, 512], P('tensor'), may hold values from -0.0625 to 0.0625
- owner_slot: int32 [64], P('rep'), parts along dimension 0, may hold values from 0 to 31, as said below
- response_length: int32 [64], P('rep'), parts along dimension 0, may hold values from 128 to 256, as said below
- pair_table: int32 [64, 2], P('rep'), parts along dimension 0, may hold values from 0 to 31, as said below
Outputs:
- judge_context: bfloat16 [64, 256, 4096], P(('rep', 'dp'), None, 'tensor'), parts along dimension 0
The draws below stay inside these ranges and needn't reach their ends.
There are 2 independent parts, one for each index of `rep`. The reference program is written for one: setup_inputs(seed, part) draws one part's arguments, and reference() takes and returns one part's arrays. A program takes and returns all parts, laid end to end along the dimension named above; an argument that names none is the same for every part. Nothing has to cross between parts.
Inputs may be any that keep to these rules, and one draw needn't show every extreme that they name: A permutation: response r is stored in row owner_slot[r] of response_states, on index owner_slot[r] // 4 of dp. `response_length`: indexed by response; rows past a response's length are padding; some response has exactly 256 tokens. `pair_table`: rows 4 * g to 4 * g + 3 are the pair tasks of index g of dp; the 8 responses named in them are distinct and stored on 8 distinct indices of dp.
All inputs are finite; a program needn't handle non-finite values.
Results may differ from the reference program's by a relative error of at most 0.008.
Values may be sent and summed in bfloat16 or wider, within the bound.
No kernel may reach another device: no remote copies, remote signals or barrier semaphores. Data moves between devices by JAX's collectives and lax.ppermute only.
A program may use at most 192 MiB of HBM per device.

```python
import jax
import jax.numpy as jnp
from jax import lax

D = 8192
HEADS = 32
KVH = 4
HD = 128
RUB = 256
PAIRS_DEV = 4
RLEN = 256
RESP_DEV = 4
RESPONSES = 32
PAIRS = 32
N_DP = 8


def shared_keys(key):
    base_key = jax.random.fold_in(key, 1000)
    normal_part = jnp.clip(jax.random.normal(base_key, (PAIRS, RUB, KVH * HD), jnp.float32), -4.0, 4.0)
    return normal_part


def owner_order(key):
    return jax.random.permutation(jax.random.fold_in(key, 2000), RESPONSES).astype(jnp.int32)


def draw_rubric_key(key, part):
    normal_part = shared_keys(key)
    return normal_part.astype(jnp.bfloat16)


def draw_rubric_query(key, part):
    own_key = jax.random.fold_in(key, 7)
    return jnp.clip(jax.random.normal(own_key, (PAIRS, RUB, HEADS * HD), jnp.float32), -4.0, 4.0).astype(jnp.bfloat16)


def draw_owner_slot(key, part):
    return owner_order(key)


def draw_response_length(key, part):
    own_key = jax.random.fold_in(key, 11)
    drawn = jax.random.randint(own_key, (RESPONSES,), RLEN // 2, RLEN + 1)
    longest = jax.random.randint(jax.random.fold_in(own_key, 1), (), 0, RESPONSES)
    return jnp.where(jnp.arange(RESPONSES) == longest, RLEN, drawn).astype(jnp.int32)


def draw_pair_table(key, part):
    own_key = jax.random.fold_in(key, 17)
    slot_of = owner_order(key)
    response_of = jnp.argsort(slot_of, stable=True).astype(jnp.int32)
    group_keys = jax.random.split(own_key, N_DP)

    def one_group(group_key):
        owner_groups = jax.random.permutation(group_key, N_DP)[:2 * PAIRS_DEV]
        picked_rows = jax.random.randint(jax.random.fold_in(group_key, 1), (2 * PAIRS_DEV,), 0, RESP_DEV)
        return response_of[owner_groups * RESP_DEV + picked_rows]
    chosen = jax.vmap(one_group)(group_keys)
    return chosen.reshape(PAIRS, 2).astype(jnp.int32)


def block_levels(key, dims, cuts, smallest, top_value):
    level = 1.0
    for axis_at, blocks in cuts:
        draws = jax.random.uniform(jax.random.fold_in(jax.random.fold_in(key, 6), axis_at), (blocks,), jnp.float32, smallest / len(cuts), top_value / len(cuts))
        level = level * jnp.repeat(jnp.exp(draws), dims[axis_at] // blocks).reshape((-1,) + (1,) * (len(dims) - 1 - axis_at))
    return level


def normal_values(key, shape, spread, reach, cuts=(), kind=jnp.bfloat16):
    factor_of = block_levels(key, shape, cuts, -0.22, 0.18) if cuts else 1.0
    entries = jax.random.normal(key, shape, jnp.float32) * spread * factor_of
    return jnp.minimum(jnp.maximum(entries, -reach), reach).astype(kind)


def setup_inputs(seed: int = 0, part: int = 0) -> dict:
    key_of = jax.random.split(jax.random.key(seed), 10)
    part_keys = jax.random.split(jax.random.fold_in(key_of[9], part), 10)
    return {
        "rubric_query": draw_rubric_query(jax.random.fold_in(jax.random.fold_in(key_of[9], part), 71), part),
        "rubric_key": draw_rubric_key(jax.random.fold_in(jax.random.fold_in(key_of[9], part), 71), part),
        "rubric_value": normal_values(part_keys[2], (PAIRS, RUB, KVH * HD), 1.0, 6.0, ((0, 8), (2, 2))),
        "response_states": normal_values(part_keys[3], (RESPONSES, RLEN, D), 1.0, 6.0, ((0, 8), (2, 2))),
        "key_weight": normal_values(key_of[4], (D, KVH * HD), D ** -0.5, 0.0625, ((0, 2),)),
        "value_weight": normal_values(key_of[5], (D, KVH * HD), D ** -0.5, 0.0625, ((0, 2),)),
        "owner_slot": draw_owner_slot(jax.random.fold_in(jax.random.fold_in(key_of[9], part), 71), part),
        "response_length": draw_response_length(jax.random.fold_in(jax.random.fold_in(key_of[9], part), 71), part),
        "pair_table": draw_pair_table(jax.random.fold_in(jax.random.fold_in(key_of[9], part), 71), part),
    }


def reference(rubric_query, rubric_key, rubric_value, response_states, key_weight, value_weight, owner_slot, response_length, pair_table):
    token_rows = response_states.reshape(RESPONSES * RLEN, D)
    keys_full = jnp.dot(token_rows, key_weight, preferred_element_type=jnp.float32).astype(jnp.bfloat16).reshape(RESPONSES, RLEN, KVH * HD)
    values_full = jnp.dot(token_rows, value_weight, preferred_element_type=jnp.float32).astype(jnp.bfloat16).reshape(RESPONSES, RLEN, KVH * HD)
    first_slot = owner_slot[pair_table[:, 0]].astype(jnp.int32)
    second_slot = owner_slot[pair_table[:, 1]].astype(jnp.int32)
    first_length = response_length[pair_table[:, 0]]
    second_length = response_length[pair_table[:, 1]]
    positions = jnp.arange(RLEN, dtype=jnp.int32)
    query_rows = jnp.arange(RUB, dtype=jnp.int32)
    causal = query_rows[:, None] >= query_rows[None, :]

    def single_pair(inputs):
        queries, own_keys, own_values, slot_first, slot_second, length_first, length_second = inputs
        stacked_keys = jnp.concatenate([keys_full[slot_first], keys_full[slot_second], own_keys], axis=0).astype(jnp.float32)
        stacked_values = jnp.concatenate([values_full[slot_first], values_full[slot_second], own_values], axis=0).astype(jnp.float32)
        query_heads = queries.astype(jnp.float32).reshape(RUB, KVH, HEADS // KVH, HD)
        key_heads = stacked_keys.reshape(-1, KVH, HD)
        value_heads = stacked_values.reshape(-1, KVH, HD)
        scores = jnp.einsum("qkgd,lkd->kgql", query_heads, key_heads) * (HD ** -0.5)
        allowed = jnp.concatenate([
            jnp.broadcast_to((positions < length_first)[None, :], (RUB, RLEN)),
            jnp.broadcast_to((positions < length_second)[None, :], (RUB, RLEN)),
            causal], axis=1)
        scores = jnp.where(allowed, scores, -1e30)
        row_peak = jnp.max(scores, axis=3, keepdims=True)
        weights_raw = jnp.where(allowed, jnp.exp(scores - row_peak), 0.0)
        denominator = jnp.sum(weights_raw, axis=3, keepdims=True)
        weights = (weights_raw / denominator).astype(jnp.bfloat16)
        context = jnp.einsum("kgql,lkd->qkgd", weights.astype(jnp.float32), value_heads)
        return context.reshape(RUB, HEADS * HD).astype(jnp.bfloat16)

    return lax.map(single_pair, (rubric_query, rubric_key, rubric_value, first_slot, second_slot, first_length, second_length))
```

```python
import functools
import math

import jax
import jax.numpy as jnp
from jax import lax
from jax.experimental import pallas as pl
from jax.experimental.pallas import tpu as pltpu
from jax.sharding import PartitionSpec as P

HD = 128
SCALE = HD ** (-0.5) * math.log2(math.e)
VMEM_LIMIT = 48 * 1024 * 1024
FIELDS = 4
HEADS_STEP = 4
SUM_ROWS = 16
IN_FLIGHT = 5
HINT = 1
ANY = pl.BlockSpec(memory_space=pl.ANY)


def params(*semantics):
    return pltpu.CompilerParams(
        dimension_semantics=semantics or None, vmem_limit_bytes=VMEM_LIMIT
    )


def hint(flops, bytes_accessed, transcendentals):
    return pl.CostEstimate(
        flops=flops // HINT,
        bytes_accessed=bytes_accessed // HINT,
        transcendentals=transcendentals // HINT,
    )


def plan_kernel(groups, stored, slots, me_ref, owner_ref, length_ref, table_ref, plan_ref):
    me = me_ref[0]

    def one(shift, carry):
        partner = lax.bitwise_xor(me, shift)
        send_row = jnp.int32(0)
        pair = jnp.int32(0)
        length = jnp.int32(0)
        wanted = jnp.int32(0)
        for j in range(slots):
            theirs = table_ref[partner * (slots // 2) + j // 2, j % 2]
            slot = owner_ref[theirs]
            send_row = jnp.where(lax.div(slot, stored) == me, lax.rem(slot, stored), send_row)
            ours = table_ref[me * (slots // 2) + j // 2, j % 2]
            hit = lax.div(owner_ref[ours], stored) == partner
            pair = jnp.where(hit, j // 2, pair)
            length = jnp.where(hit, length_ref[ours], length)
            wanted = jnp.where(hit, 1, wanted)
        plan_ref[shift * FIELDS] = send_row
        plan_ref[shift * FIELDS + 1] = pair
        plan_ref[shift * FIELDS + 2] = length
        plan_ref[shift * FIELDS + 3] = wanted
        return carry

    lax.fori_loop(0, groups, one, 0)


def make_plan(me, owner_slot, response_length, pair_table, groups, stored, pairs):
    smem = pl.BlockSpec(memory_space=pltpu.SMEM)
    return pl.pallas_call(
        functools.partial(plan_kernel, groups, stored, 2 * pairs),
        out_shape=jax.ShapeDtypeStruct((groups * FIELDS,), jnp.int32),
        in_specs=[smem] * 4,
        out_specs=smem,
        name="plan",
    )(me, owner_slot, response_length, pair_table)


def project_kernel(half_ref, x_ref, key_ref, value_ref, *refs):
    out_ref = refs[-1]
    width = key_ref.shape[1]
    x = x_ref[...]
    for at, weight_ref in enumerate((key_ref, value_ref)):
        columns = slice(at * width, (at + 1) * width)
        part = jnp.dot(x, weight_ref[...], preferred_element_type=jnp.float32)

        @pl.when(pl.program_id(0) == 0)
        def _():
            out_ref[:, columns] = part

        @pl.when(pl.program_id(0) > 0)
        def _():
            out_ref[:, columns] += part


def project(rows, key_weight, value_weight, half, width, name, after=()):
    total, depth = rows.shape
    chunk = 512
    weight_spec = pl.BlockSpec((chunk, width), lambda k, half: (k, half[0]))
    return pl.pallas_call(
        project_kernel,
        grid_spec=pltpu.PrefetchScalarGridSpec(
            num_scalar_prefetch=1,
            grid=(depth // chunk,),
            in_specs=[pl.BlockSpec((total, chunk), lambda k, half: (0, k)), weight_spec, weight_spec]
            + [ANY] * len(after),
            out_specs=pl.BlockSpec((total, 2 * width), lambda k, half: (0, 0)),
        ),
        out_shape=jax.ShapeDtypeStruct((total, 2 * width), jnp.float32),
        compiler_params=params("arbitrary"),
        cost_estimate=hint(
            4 * total * depth * width, 2 * total * depth + 4 * depth * width + 8 * total * width, 0
        ),
        name=name,
    )(half, rows, key_weight, value_weight, *after)


def finish_kernel(length, width, plan_ref, own_ref, other_ref, *out_refs):
    for shift, out_ref in enumerate(out_refs):
        start = pl.multiple_of(plan_ref[shift * FIELDS] * length, length)
        rows = pl.ds(start, length)
        for at in range(2):
            columns = slice(at * width, (at + 1) * width)
            total = own_ref[rows, columns] + other_ref[rows, columns]
            out_ref[at * length : (at + 1) * length, :] = total.astype(out_ref.dtype)


def finish(plan, own, other, groups, length, name):
    width = own.shape[1] // 2
    vmem = pl.BlockSpec(memory_space=pltpu.VMEM)
    return pl.pallas_call(
        functools.partial(finish_kernel, length, width),
        out_shape=[jax.ShapeDtypeStruct((2 * length, width), jnp.bfloat16)] * groups,
        in_specs=[pl.BlockSpec(memory_space=pltpu.SMEM), vmem, vmem],
        out_specs=[vmem] * groups,
        compiler_params=params(),
        cost_estimate=hint(
            2 * groups * length * width,
            16 * own.shape[0] * width + 4 * groups * length * width,
            0,
        ),
        name=name,
    )(plan, own, other)


def scores_of(keys, queries):
    return lax.dot_general(
        keys, queries, (((1,), (1,)), ((), ())), preferred_element_type=jnp.float32
    )


def rubric_kernel(q_ref, k_ref, v_ref, *refs):
    acc_ref, ml_ref = refs[-2:]
    keys = k_ref[0]
    count = keys.shape[0]
    values = jnp.concatenate(
        [v_ref[0].T, jnp.ones((SUM_ROWS, count), jnp.bfloat16)], axis=0
    )
    shape = (count, q_ref.shape[1])
    causal = lax.broadcasted_iota(jnp.int32, shape, 0) <= lax.broadcasted_iota(jnp.int32, shape, 1)
    for h in range(HEADS_STEP):
        s = scores_of(keys, q_ref[0, :, h * HD : (h + 1) * HD])
        s = jnp.where(causal, s, -1e30)
        peak = jnp.max(s, axis=0, keepdims=True)
        weights = jnp.exp2((s - peak) * SCALE).astype(jnp.bfloat16)
        pv = jnp.dot(values, weights, preferred_element_type=jnp.float32)
        acc_ref[0, h * HD : (h + 1) * HD, :] = pv[:HD]
        ml_ref[0, 0, h : h + 1, :] = peak
        ml_ref[0, 0, HEADS_STEP + h : HEADS_STEP + h + 1, :] = pv[HD : HD + 1]


def rubric_attention(first, some, query, key, value, state, after=()):
    pairs, rows, width = query.shape
    heads = width // HD
    steps = heads // HEADS_STEP
    per_head = steps * HD // key.shape[2]
    step_width = HEADS_STEP * HD
    count = key.shape[1]
    return pl.pallas_call(
        rubric_kernel,
        grid=(some, steps),
        in_specs=[
            pl.BlockSpec((1, rows, step_width), lambda p, g: (first + p, 0, g)),
            pl.BlockSpec((1, count, HD), lambda p, g: (first + p, 0, g // per_head)),
            pl.BlockSpec((1, count, HD), lambda p, g: (first + p, 0, g // per_head)),
        ]
        + [ANY] * (len(state) + len(after)),
        out_specs=[
            pl.BlockSpec((1, step_width, rows), lambda p, g: (first + p, g, 0)),
            pl.BlockSpec((1, 1, 2 * HEADS_STEP, rows), lambda p, g: (first + p, g, 0, 0)),
        ],
        out_shape=[
            jax.ShapeDtypeStruct((pairs, width, rows), jnp.float32),
            jax.ShapeDtypeStruct((pairs, steps, 2 * HEADS_STEP, rows), jnp.float32),
        ],
        input_output_aliases={3: 0, 4: 1} if state else {},
        compiler_params=params("arbitrary", "arbitrary"),
        cost_estimate=hint(4 * some * heads * rows * count * HD, some * rows * width * 6, some * heads * rows * count),
        name="rubric_attention",
    )(query, key, value, *state, *after)


def response_kernel(shift, per_head, plan_ref, q_ref, kv_ref, acc_ref, ml_ref, *refs):
    acc_out, ml_out, out_ref, keys_ref, values_ref = refs[-5:]
    count = kv_ref.shape[0] // 2
    kv_heads = kv_ref.shape[1] // HD
    length = plan_ref[shift * FIELDS + 2]
    wanted = plan_ref[shift * FIELDS + 3] == 1
    step = pl.program_id(0)

    @pl.when(step == 0)
    def _():
        live_rows = lax.broadcasted_iota(jnp.int32, (count, HD), 0) < length
        live_columns = lax.broadcasted_iota(jnp.int32, (HD + SUM_ROWS, count), 1) < length
        for kv in range(kv_heads):
            columns = slice(kv * HD, (kv + 1) * HD)
            block = kv_ref[:count, columns].astype(jnp.float32)
            keys_ref[kv] = jnp.where(live_rows, block, block[0:1]).astype(jnp.bfloat16)
            block = kv_ref[count:, columns].astype(jnp.float32)
            values = jnp.concatenate(
                [block.T, jnp.ones((SUM_ROWS, count), jnp.float32)], axis=0
            )
            values_ref[kv] = jnp.where(live_columns, values, 0.0).astype(jnp.bfloat16)

    def emit(h, acc, total):
        out_ref[0, :, h * HD : (h + 1) * HD] = (acc * (1.0 / total)).T.astype(out_ref.dtype)

    @pl.when(wanted)
    def _():
        keys = keys_ref[step // per_head]
        values = values_ref[step // per_head]
        for h in range(HEADS_STEP):
            head = slice(h * HD, (h + 1) * HD)
            peak_row = slice(h, h + 1)
            total_row = slice(HEADS_STEP + h, HEADS_STEP + h + 1)
            s = scores_of(keys, q_ref[0, :, head])
            old_peak = ml_ref[0, 0, peak_row, :]
            peak = jnp.maximum(old_peak, jnp.max(s, axis=0, keepdims=True))
            weights = jnp.exp2((s - peak) * SCALE).astype(jnp.bfloat16)
            fade = jnp.exp2((old_peak - peak) * SCALE)
            pv = jnp.dot(values, weights, preferred_element_type=jnp.float32)
            acc = acc_ref[0, head, :] * fade + pv[:HD]
            total = ml_ref[0, 0, total_row, :] * fade + pv[HD : HD + 1]
            acc_out[0, head, :] = acc
            ml_out[0, 0, peak_row, :] = peak
            ml_out[0, 0, total_row, :] = total
            emit(h, acc, total)

    @pl.when(jnp.logical_not(wanted))
    def _():
        acc_out[...] = acc_ref[...]
        ml_out[...] = ml_ref[...]
        for h in range(HEADS_STEP):
            emit(
                h,
                acc_ref[0, h * HD : (h + 1) * HD, :],
                ml_ref[0, 0, HEADS_STEP + h : HEADS_STEP + h + 1, :],
            )


def response_attention(shift, plan, query, kv, acc, ml, out):
    pairs, rows, width = query.shape
    heads = width // HD
    steps = heads // HEADS_STEP
    per_head = steps * HD // kv.shape[1]
    step_width = HEADS_STEP * HD
    count = kv.shape[0] // 2
    pair_at = shift * FIELDS + 1
    acc_spec = pl.BlockSpec((1, step_width, rows), lambda g, plan: (plan[pair_at], g, 0))
    ml_spec = pl.BlockSpec((1, 1, 2 * HEADS_STEP, rows), lambda g, plan: (plan[pair_at], g, 0, 0))
    row_spec = pl.BlockSpec((1, rows, step_width), lambda g, plan: (plan[pair_at], 0, g))
    operands = [plan, query, kv, acc, ml]
    in_specs = [row_spec, pl.BlockSpec(kv.shape, lambda g, plan: (0, 0)), acc_spec, ml_spec]
    aliases = {3: 0, 4: 1}
    if out is not None:
        operands.append(out)
        in_specs.append(pl.BlockSpec(memory_space=pl.ANY))
        aliases[5] = 2
    return pl.pallas_call(
        functools.partial(response_kernel, shift, per_head),
        grid_spec=pltpu.PrefetchScalarGridSpec(
            num_scalar_prefetch=1,
            grid=(steps,),
            in_specs=in_specs,
            out_specs=[acc_spec, ml_spec, row_spec],
            scratch_shapes=[
                pltpu.VMEM((kv.shape[1] // HD, count, HD), jnp.bfloat16),
                pltpu.VMEM((kv.shape[1] // HD, HD + SUM_ROWS, count), jnp.bfloat16),
            ],
        ),
        out_shape=[
            jax.ShapeDtypeStruct(acc.shape, acc.dtype),
            jax.ShapeDtypeStruct(ml.shape, ml.dtype),
            jax.ShapeDtypeStruct(query.shape, jnp.bfloat16),
        ],
        input_output_aliases=aliases,
        compiler_params=params("arbitrary"),
        cost_estimate=hint(4 * heads * rows * count * HD, rows * width * 12, heads * rows * count),
        name="response_attention",
    )(*operands)


def local(
    rubric_query,
    rubric_key,
    rubric_value,
    response_states,
    key_weight,
    value_weight,
    owner_slot,
    response_length,
    pair_table,
):
    groups = lax.axis_size("dp")
    stored, length, depth = response_states.shape
    pairs = rubric_query.shape[0]
    tensor = lax.axis_size("tensor")
    width = key_weight.shape[1] // tensor
    me = lax.axis_index("dp").astype(jnp.int32)
    own_half = lax.axis_index("tensor").astype(jnp.int32)
    other_half = 1 - own_half
    rows = response_states.reshape(stored * length, depth)
    swap = [(0, 1), (1, 0)]
    plan = make_plan(
        me[None], owner_slot, response_length, pair_table, groups, stored, pairs
    )

    other = project(rows, key_weight, value_weight, other_half[None], width, "other_half")
    received = lax.ppermute(other, "tensor", swap)
    own = project(rows, key_weight, value_weight, own_half[None], width, "own_half", after=[other])
    blocks = finish(plan, own, received, groups, length, "finish")

    far = list(range(groups - 1, groups // 2 - 1, -1))
    near = list(range(groups // 2 - 1, 0, -1))
    order = []
    for at in range(len(far)):
        order += far[at : at + 1] + near[at : at + 1]
    arrived = {}

    def send(shift, *after):
        block = lax.optimization_barrier((blocks[shift], *after))[0]
        arrived[shift] = lax.ppermute(block, "dp", [(g, g ^ shift) for g in range(groups)])

    for shift in order[:IN_FLIGHT]:
        send(shift)
    state = rubric_attention(
        0, pairs, rubric_query, rubric_key, rubric_value, (), after=[blocks[0]]
    )
    acc, ml, out = response_attention(0, plan, rubric_query, blocks[0], *state, None)
    for at, shift in enumerate(order):
        if at + IN_FLIGHT < len(order):
            send(order[at + IN_FLIGHT], arrived[shift], ml)
        acc, ml, out = response_attention(shift, plan, rubric_query, arrived[shift], acc, ml, out)
    return out


def solution(mesh):
    return jax.shard_map(
        local,
        mesh=mesh,
        in_specs=(
            P(("rep", "dp"), None, "tensor"),
            P(("rep", "dp"), None, "tensor"),
            P(("rep", "dp"), None, "tensor"),
            P(("rep", "dp"), None, "tensor"),
            P("tensor", None),
            P("tensor", None),
            P("rep"),
            P("rep"),
            P("rep", None),
        ),
        out_specs=P(("rep", "dp"), None, "tensor"),
        check_vma=False,
    )
```

```python
import functools
import math

import jax
import jax.numpy as jnp
from jax import lax
from jax.experimental import pallas as pl
from jax.experimental.pallas import tpu as pltpu
from jax.sharding import PartitionSpec as P

HD = 128
SCALE = HD ** (-0.5) * math.log2(math.e)
MIB = 1024 * 1024
FIELDS = 5
SUM_ROWS = 16
IN_FLIGHT = 5
NEVER = -1e30
ANY = pl.BlockSpec(memory_space=pl.ANY)
SMEM = pl.BlockSpec(memory_space=pltpu.SMEM)
WHOLE = pl.BlockSpec(memory_space=pltpu.VMEM)


def params(*semantics, vmem=24):
    return pltpu.CompilerParams(
        dimension_semantics=semantics or None, vmem_limit_bytes=vmem * MIB
    )


def hint(flops, bytes_accessed, transcendentals):
    return pl.CostEstimate(
        flops=flops, bytes_accessed=bytes_accessed, transcendentals=transcendentals
    )


def arrival_order(groups):
    far = list(range(groups - 1, groups // 2 - 1, -1))
    near = list(range(groups // 2 - 1, 0, -1))
    order = [0]
    for at in range(len(far)):
        order += far[at : at + 1] + near[at : at + 1]
    return order


def write_plan(groups, stored, me, owner_ref, length_ref, table_ref, place_ref, plan_ref):
    pairs = table_ref.shape[1] // groups
    bits = stored.bit_length() - 1

    def slot_of(group, j):
        response = table_ref[j % 2, group * pairs + j // 2]
        slot = owner_ref[response]
        return response, lax.shift_right_logical(slot, bits), slot & (stored - 1)

    for shift in range(groups):
        plan_ref[shift * FIELDS + 3] = 0
        plan_ref[shift * FIELDS + 1] = 0
        row = jnp.int32(0)
        for j in range(2 * pairs):
            _, source, slot_row = slot_of(me ^ shift, j)
            row = jnp.where(source == me, slot_row, row)
        plan_ref[shift * FIELDS] = row
    sources = [slot_of(me, j) for j in range(2 * pairs)]
    for j, (response, source, _) in enumerate(sources):
        shift = source ^ me
        later = place_ref[shift] > place_ref[sources[j ^ 1][1] ^ me]
        plan_ref[shift * FIELDS + 1] = jnp.int32(j // 2)
        plan_ref[shift * FIELDS + 2] = length_ref[response]
        plan_ref[shift * FIELDS + 3] = jnp.int32(1)
        plan_ref[shift * FIELDS + 4] = later.astype(jnp.int32)


def project_rows_kernel(groups, stored, at_ref, owner_ref, length_ref, table_ref, place_ref, x_ref, key_ref, value_ref, out_ref, plan_ref):
    write_plan(groups, stored, at_ref[1], owner_ref, length_ref, table_ref, place_ref, plan_ref)
    width = key_ref.shape[1]
    x = x_ref[...]
    out_ref[:, :width] = jnp.dot(x, key_ref[...], preferred_element_type=jnp.float32)
    out_ref[:, width:] = jnp.dot(x, value_ref[...], preferred_element_type=jnp.float32)


def project_and_plan(rows, key_weight, value_weight, half, width, me, tables, groups, stored):
    total, depth = rows.shape
    block = 256
    weight_spec = pl.BlockSpec((depth, width), lambda i, at: (0, at[0]))
    return pl.pallas_call(
        functools.partial(project_rows_kernel, groups, stored),
        grid_spec=pltpu.PrefetchScalarGridSpec(
            num_scalar_prefetch=1,
            grid=(total // block,),
            in_specs=[SMEM] * len(tables)
            + [pl.BlockSpec((block, depth), lambda i, at: (i, 0)), weight_spec, weight_spec],
            out_specs=[pl.BlockSpec((block, 2 * width), lambda i, at: (i, 0)), SMEM],
        ),
        out_shape=[
            jax.ShapeDtypeStruct((total, 2 * width), jnp.float32),
            jax.ShapeDtypeStruct((groups * FIELDS,), jnp.int32),
        ],
        compiler_params=params("arbitrary", vmem=60),
        cost_estimate=hint(
            4 * total * depth * width, 2 * total * depth + 4 * depth * width + 8 * total * width, 0
        ),
        name="other_half",
    )(jnp.stack([half, me]), *tables, rows, key_weight, value_weight)


def project_kernel(half_ref, x_ref, key_ref, value_ref, *refs):
    out_ref = refs[-1]
    width = key_ref.shape[1]
    x = x_ref[...]
    for at, weight_ref in enumerate((key_ref, value_ref)):
        columns = slice(at * width, (at + 1) * width)
        part = jnp.dot(x, weight_ref[...], preferred_element_type=jnp.float32)

        @pl.when(pl.program_id(0) == 0)
        def _():
            out_ref[:, columns] = part

        @pl.when(pl.program_id(0) > 0)
        def _():
            out_ref[:, columns] += part


def project(rows, key_weight, value_weight, half, width, name, after=()):
    total, depth = rows.shape
    chunk = 1024
    weight_spec = pl.BlockSpec((chunk, width), lambda k, half: (k, half[0]))
    return pl.pallas_call(
        project_kernel,
        grid_spec=pltpu.PrefetchScalarGridSpec(
            num_scalar_prefetch=1,
            grid=(depth // chunk,),
            in_specs=[pl.BlockSpec((total, chunk), lambda k, half: (0, k)), weight_spec, weight_spec]
            + [ANY] * len(after),
            out_specs=pl.BlockSpec((total, 2 * width), lambda k, half: (0, 0)),
        ),
        out_shape=jax.ShapeDtypeStruct((total, 2 * width), jnp.float32),
        compiler_params=params("arbitrary", vmem=48),
        cost_estimate=hint(
            4 * total * depth * width, 2 * total * depth + 4 * depth * width + 8 * total * width, 0
        ),
        name=name,
    )(half[None], rows, key_weight, value_weight, *after)


def finish_kernel(length, width, plan_ref, own_ref, other_ref, *out_refs):
    for shift, out_ref in enumerate(out_refs):
        start = pl.multiple_of(plan_ref[shift * FIELDS] * length, length)
        rows = pl.ds(start, length)
        for at in range(2):
            columns = slice(at * width, (at + 1) * width)
            total = own_ref[rows, columns] + other_ref[rows, columns]
            out_ref[at * length : (at + 1) * length, :] = total.astype(out_ref.dtype)


def finish(plan, own, other, groups, length, name):
    width = own.shape[1] // 2
    return pl.pallas_call(
        functools.partial(finish_kernel, length, width),
        out_shape=[jax.ShapeDtypeStruct((2 * length, width), jnp.bfloat16)] * groups,
        in_specs=[SMEM, WHOLE, WHOLE],
        out_specs=[WHOLE] * groups,
        compiler_params=params(),
        cost_estimate=hint(
            2 * groups * length * width,
            16 * own.shape[0] * width + 4 * groups * length * width,
            0,
        ),
        name=name,
    )(plan, own, other)


def times(a, b):
    return jnp.dot(a, b, preferred_element_type=jnp.float32)


def head_rows(h):
    return slice(h * HD, (h + 1) * HD)


def softmax_part(s, peak):
    return jnp.exp2((s - peak) * SCALE).astype(jnp.bfloat16)


def top_of(s):
    return jnp.max(s, axis=0, keepdims=True)


def rubric_kernel(q_ref, k_ref, v_ref, after_ref, qt_ref, acc_ref, peak_ref, sum_ref):
    heads = qt_ref.shape[1] // HD
    half = k_ref.shape[1] // 2
    keys = k_ref[0]
    values = jnp.concatenate(
        [v_ref[0].T, jnp.ones((SUM_ROWS, 2 * half), jnp.bfloat16)], axis=0
    )
    shape = (half, half)
    causal = lax.broadcasted_iota(jnp.int32, shape, 0) <= lax.broadcasted_iota(jnp.int32, shape, 1)

    def scores(h):
        turned = q_ref[0, :, head_rows(h)].T
        qt_ref[0, head_rows(h), :] = turned
        return times(keys[:half], turned), times(keys[half:], turned[:, half:])

    later = scores(0)
    for h in range(heads):
        first, last = later
        if h + 1 < heads:
            later = scores(h + 1)
        early = jnp.where(causal, first[:, :half], NEVER)
        late = first[:, half:]
        last = jnp.where(causal, last, NEVER)
        early_peak = top_of(early)
        late_peak = jnp.maximum(top_of(late), top_of(last))
        weights = jnp.concatenate(
            [softmax_part(early, early_peak), softmax_part(late, late_peak)], axis=1
        )
        pv = times(values[:, :half], weights)
        more = times(values[:, half:], softmax_part(last, late_peak))
        acc_ref[0, head_rows(h), :half] = pv[:HD, :half]
        acc_ref[0, head_rows(h), half:] = pv[:HD, half:] + more[:HD]
        peak_ref[0, h : h + 1, :half] = early_peak
        peak_ref[0, h : h + 1, half:] = late_peak
        sum_ref[0, h : h + 1, :half] = pv[HD : HD + 1, :half]
        sum_ref[0, h : h + 1, half:] = pv[HD : HD + 1, half:] + more[HD : HD + 1]


def state_shapes(pairs, rows, width):
    heads = width // HD
    return [
        jax.ShapeDtypeStruct((pairs, width, rows), jnp.bfloat16),
        jax.ShapeDtypeStruct((pairs, width, rows), jnp.float32),
        jax.ShapeDtypeStruct((pairs, heads, rows), jnp.float32),
        jax.ShapeDtypeStruct((pairs, heads, rows), jnp.float32),
    ]


def rubric_attention(query, key, value, after):
    pairs, rows, width = query.shape
    steps = key.shape[2] // HD
    step_width = width // steps
    heads = width // HD
    count = key.shape[1]

    def spec(size):
        return pl.BlockSpec((1, size, rows), lambda p, g: (p, g, 0))

    def across(size):
        return pl.BlockSpec((1, rows, size), lambda p, g: (p, 0, g))

    return pl.pallas_call(
        rubric_kernel,
        grid=(pairs, steps),
        in_specs=[across(step_width), across(HD), across(HD), ANY],
        out_specs=[spec(step_width), spec(step_width), spec(heads // steps), spec(heads // steps)],
        out_shape=state_shapes(pairs, rows, width),
        compiler_params=params("arbitrary", "arbitrary"),
        cost_estimate=hint(
            3 * pairs * heads * rows * count * HD,
            pairs * rows * width * 8,
            pairs * heads * rows * count,
        ),
        name="rubric_attention",
    )(query, key, value, after)


def response_kernel(shift, plan_ref, qt_ref, kv_ref, acc_ref, peak_ref, sum_ref, *refs):
    acc_out, peak_out, sum_out, out_ref = refs[-4:]
    heads = qt_ref.shape[1] // HD
    count = kv_ref.shape[0] // 2
    length = plan_ref[shift * FIELDS + 2]
    wanted = plan_ref[shift * FIELDS + 3] == 1
    completes = plan_ref[shift * FIELDS + 4] == 1

    @pl.when(wanted)
    def _():
        live_rows = lax.broadcasted_iota(jnp.int32, (count, HD), 0) < length
        live_columns = lax.broadcasted_iota(jnp.int32, (HD + SUM_ROWS, count), 1) < length
        block = kv_ref[:count, :].astype(jnp.float32)
        keys = jnp.where(live_rows, block, block[0:1]).astype(jnp.bfloat16)
        values = jnp.concatenate(
            [kv_ref[count:, :].astype(jnp.float32).T, jnp.ones((SUM_ROWS, count), jnp.float32)],
            axis=0,
        )
        values = jnp.where(live_columns, values, 0.0).astype(jnp.bfloat16)
        later = times(keys, qt_ref[0, head_rows(0), :])
        for h in range(heads):
            s = later
            if h + 1 < heads:
                later = times(keys, qt_ref[0, head_rows(h + 1), :])
            old_peak = peak_ref[0, h : h + 1, :]
            peak = jnp.maximum(old_peak, top_of(s))
            fade = jnp.exp2((old_peak - peak) * SCALE)
            pv = times(values, softmax_part(s, peak))
            acc_out[0, head_rows(h), :] = acc_ref[0, head_rows(h), :] * fade + pv[:HD]
            peak_out[0, h : h + 1, :] = peak
            sum_out[0, h : h + 1, :] = sum_ref[0, h : h + 1, :] * fade + pv[HD : HD + 1]

    @pl.when(jnp.logical_not(wanted))
    def _():
        acc_out[...] = acc_ref[...]
        peak_out[...] = peak_ref[...]
        sum_out[...] = sum_ref[...]

    @pl.when(completes | jnp.logical_not(wanted))
    def _():
        for h in range(heads):
            share = acc_out[0, head_rows(h), :] * (1.0 / sum_out[0, h : h + 1, :])
            out_ref[0, :, head_rows(h)] = share.astype(out_ref.dtype).T


def response_attention(shift, plan, kv, state, out):
    pairs, width, rows = state[0].shape
    heads = width // HD
    steps = kv.shape[1] // HD
    step_width = width // steps
    count = kv.shape[0] // 2
    pair_at = shift * FIELDS + 1

    def spec(size):
        return pl.BlockSpec((1, size, rows), lambda g, plan: (plan[pair_at], g, 0))

    state_specs = [spec(step_width), spec(heads // steps), spec(heads // steps)]
    operands = [plan, state[0], kv, *state[1:]]
    in_specs = [
        spec(step_width),
        pl.BlockSpec((2 * count, HD), lambda g, plan: (0, g)),
        *state_specs,
    ]
    aliases = {3: 0, 4: 1, 5: 2}
    if out is not None:
        aliases[len(operands)] = 3
        operands.append(out)
        in_specs.append(ANY)
    results = pl.pallas_call(
        functools.partial(response_kernel, shift),
        grid_spec=pltpu.PrefetchScalarGridSpec(
            num_scalar_prefetch=1,
            grid=(steps,),
            in_specs=in_specs,
            out_specs=state_specs
            + [pl.BlockSpec((1, rows, step_width), lambda g, plan: (plan[pair_at], 0, g))],
        ),
        out_shape=state_shapes(pairs, rows, width)[1:]
        + [jax.ShapeDtypeStruct((pairs, rows, width), jnp.bfloat16)],
        input_output_aliases=aliases,
        compiler_params=params("arbitrary"),
        cost_estimate=hint(
            4 * heads * rows * count * HD, rows * width * 12, heads * rows * count
        ),
        name="response_attention",
    )(*operands)
    return [state[0], *results[:3]], results[3]


def local(
    rubric_query,
    rubric_key,
    rubric_value,
    response_states,
    key_weight,
    value_weight,
    owner_slot,
    response_length,
    pair_table,
):
    groups = lax.axis_size("dp")
    stored, length, depth = response_states.shape
    tensor = lax.axis_size("tensor")
    width = key_weight.shape[1] // tensor
    me = lax.axis_index("dp").astype(jnp.int32)
    own_half = lax.axis_index("tensor").astype(jnp.int32)
    other_half = 1 - own_half
    rows = response_states.reshape(stored * length, depth)
    swap = [(0, 1), (1, 0)]
    order = arrival_order(groups)
    place = jnp.array([order.index(shift) for shift in range(groups)], jnp.int32)
    tables = [owner_slot, response_length, pair_table.T, place]

    other, plan = project_and_plan(
        rows, key_weight, value_weight, other_half, width, me, tables, groups, stored
    )
    received = lax.ppermute(other, "tensor", swap)
    own = project(rows, key_weight, value_weight, own_half, width, "own_half", after=[plan])
    blocks = finish(plan, own, received, groups, length, "finish")
    arrived = {0: blocks[0]}

    def send(shift, *after):
        block = lax.optimization_barrier((blocks[shift], *after))[0]
        arrived[shift] = lax.ppermute(block, "dp", [(g, g ^ shift) for g in range(groups)])

    for shift in order[1 : IN_FLIGHT + 1]:
        send(shift)
    state = rubric_attention(rubric_query, rubric_key, rubric_value, blocks[0])
    out = None
    for at, shift in enumerate(order):
        if at and at + IN_FLIGHT < len(order):
            send(order[at + IN_FLIGHT], arrived[shift], state[2])
        state, out = response_attention(shift, plan, arrived[shift], state, out)
    return out


def solution(mesh):
    return jax.shard_map(
        local,
        mesh=mesh,
        in_specs=(
            P(("rep", "dp"), None, "tensor"),
            P(("rep", "dp"), None, "tensor"),
            P(("rep", "dp"), None, "tensor"),
            P(("rep", "dp"), None, "tensor"),
            P("tensor", None),
            P("tensor", None),
            P("rep"),
            P("rep"),
            P("rep", None),
        ),
        out_specs=P(("rep", "dp"), None, "tensor"),
        check_vma=False,
    )
```

```python
import functools
import math

import jax
import jax.numpy as jnp
from jax import lax
from jax.experimental import pallas as pl
from jax.experimental.pallas import tpu as pltpu
from jax.sharding import PartitionSpec as P

HD = 128
SCALE = HD ** (-0.5) * math.log2(math.e)
MIB = 1024 * 1024
FIELDS = 5
SUM_ROWS = 16
SUB_ROWS = 128
NEVER = -1e30
ANY = pl.BlockSpec(memory_space=pl.ANY)
SMEM = pl.BlockSpec(memory_space=pltpu.SMEM)
WHOLE = pl.BlockSpec(memory_space=pltpu.VMEM)


def params(*semantics, vmem=24):
    return pltpu.CompilerParams(
        dimension_semantics=semantics or None, vmem_limit_bytes=vmem * MIB
    )


def hint(flops, bytes_accessed, transcendentals):
    return pl.CostEstimate(
        flops=flops, bytes_accessed=bytes_accessed, transcendentals=transcendentals
    )


def arrival_order(groups):
    far = list(range(groups - 1, groups // 2 - 1, -1))
    near = list(range(groups // 2 - 1, 0, -1))
    order = []
    for at in range(len(far)):
        order += far[at : at + 1] + near[at : at + 1]
    return order


def write_plan(groups, stored, me, owner_ref, length_ref, table_ref, place_ref, plan_ref):
    pairs = table_ref.shape[1] // groups
    bits = stored.bit_length() - 1

    def slot_of(group, j):
        response = table_ref[j % 2, group * pairs + j // 2]
        slot = owner_ref[response]
        return response, lax.shift_right_logical(slot, bits), slot & (stored - 1)

    for shift in range(groups):
        plan_ref[shift * FIELDS + 3] = 0
        plan_ref[shift * FIELDS + 1] = 0
        row = jnp.int32(0)
        for j in range(2 * pairs):
            _, source, slot_row = slot_of(me ^ shift, j)
            row = jnp.where(source == me, slot_row, row)
        plan_ref[shift * FIELDS] = row
    sources = [slot_of(me, j) for j in range(2 * pairs)]
    for j, (response, source, _) in enumerate(sources):
        shift = source ^ me
        later = place_ref[shift] > place_ref[sources[j ^ 1][1] ^ me]
        plan_ref[shift * FIELDS + 1] = jnp.int32(j // 2)
        plan_ref[shift * FIELDS + 2] = length_ref[response]
        plan_ref[shift * FIELDS + 3] = jnp.int32(1)
        plan_ref[shift * FIELDS + 4] = later.astype(jnp.int32)


def project_rows_kernel(groups, stored, half_ref, me_ref, owner_ref, length_ref, table_ref, place_ref, x_ref, key_ref, value_ref, out_ref, plan_ref):
    write_plan(groups, stored, me_ref[0], owner_ref, length_ref, table_ref, place_ref, plan_ref)
    width = key_ref.shape[1]
    for at in range(0, x_ref.shape[0], SUB_ROWS):
        part = slice(at, at + SUB_ROWS)
        out_ref[part, :width] = times(x_ref[part, :], key_ref[...])
        out_ref[part, width:] = times(x_ref[part, :], value_ref[...])


def project_and_plan(rows, key_weight, value_weight, half, width, me, tables, groups, stored):
    total, depth = rows.shape
    block = 256
    weight_spec = pl.BlockSpec((depth, width), lambda i, half, me: (0, half[0]))
    return pl.pallas_call(
        functools.partial(project_rows_kernel, groups, stored),
        grid_spec=pltpu.PrefetchScalarGridSpec(
            num_scalar_prefetch=2,
            grid=(total // block,),
            in_specs=[SMEM] * len(tables)
            + [pl.BlockSpec((block, depth), lambda i, half, me: (i, 0)), weight_spec, weight_spec],
            out_specs=[pl.BlockSpec((block, 2 * width), lambda i, half, me: (i, 0)), SMEM],
        ),
        out_shape=[
            jax.ShapeDtypeStruct((total, 2 * width), jnp.float32),
            jax.ShapeDtypeStruct((groups * FIELDS,), jnp.int32),
        ],
        compiler_params=params("arbitrary", vmem=60),
        cost_estimate=hint(
            4 * total * depth * width, 2 * total * depth + 4 * depth * width + 8 * total * width, 0
        ),
        name="other_half",
    )(half[None], me[None], *tables, rows, key_weight, value_weight)


def finish_kernel(length, width, plan_ref, own_keys_ref, own_values_ref, other_ref, *out_refs):
    for shift, out_ref in enumerate(out_refs):
        start = pl.multiple_of(plan_ref[shift * FIELDS] * length, length)
        rows = pl.ds(start, length)
        for at, own_ref in enumerate((own_keys_ref, own_values_ref)):
            total = own_ref[rows, :] + other_ref[rows, at * width : (at + 1) * width]
            out_ref[at * length : (at + 1) * length, :] = total.astype(out_ref.dtype)


def finish(plan, own_keys, own_values, other, groups, length, name):
    total, width = own_keys.shape
    return pl.pallas_call(
        functools.partial(finish_kernel, length, width),
        out_shape=[jax.ShapeDtypeStruct((2 * length, width), jnp.bfloat16)] * groups,
        in_specs=[SMEM, WHOLE, WHOLE, WHOLE],
        out_specs=[WHOLE] * groups,
        compiler_params=params(),
        cost_estimate=hint(
            2 * groups * length * width,
            16 * total * width + 4 * groups * length * width,
            0,
        ),
        name=name,
    )(plan, own_keys, own_values, other)


def times(a, b):
    return jnp.dot(a, b, preferred_element_type=jnp.float32)


def head_rows(h):
    return slice(h * HD, (h + 1) * HD)


def softmax_part(s, peak):
    return jnp.exp2((s - peak) * SCALE).astype(jnp.bfloat16)


def top_of(s):
    return jnp.max(s, axis=0, keepdims=True)


def rubric_kernel(q_ref, k_ref, v_ref, *refs):
    qt_ref, acc_ref, peak_ref, sum_ref = refs[-4:]
    heads = qt_ref.shape[1] // HD
    half = k_ref.shape[1] // 2
    keys = k_ref[0]
    values = jnp.concatenate(
        [v_ref[0].T, jnp.ones((SUM_ROWS, 2 * half), jnp.bfloat16)], axis=0
    )
    shape = (half, half)
    causal = lax.broadcasted_iota(jnp.int32, shape, 0) <= lax.broadcasted_iota(jnp.int32, shape, 1)

    def scores(h):
        turned = q_ref[0, :, head_rows(h)].T
        qt_ref[0, head_rows(h), :] = turned
        return times(keys[:half], turned), times(keys[half:], turned[:, half:])

    later = scores(0)
    for h in range(heads):
        first, last = later
        if h + 1 < heads:
            later = scores(h + 1)
        early = jnp.where(causal, first[:, :half], NEVER)
        late = first[:, half:]
        last = jnp.where(causal, last, NEVER)
        early_peak = top_of(early)
        late_peak = jnp.maximum(top_of(late), top_of(last))
        weights = jnp.concatenate(
            [softmax_part(early, early_peak), softmax_part(late, late_peak)], axis=1
        )
        pv = times(values[:, :half], weights)
        more = times(values[:, half:], softmax_part(last, late_peak))
        acc_ref[0, head_rows(h), :half] = pv[:HD, :half]
        acc_ref[0, head_rows(h), half:] = pv[:HD, half:] + more[:HD]
        peak_ref[0, h : h + 1, :half] = early_peak
        peak_ref[0, h : h + 1, half:] = late_peak
        sum_ref[0, h : h + 1, :half] = pv[HD : HD + 1, :half]
        sum_ref[0, h : h + 1, half:] = pv[HD : HD + 1, half:] + more[HD : HD + 1]


def state_shapes(pairs, rows, width):
    heads = width // HD
    return [
        jax.ShapeDtypeStruct((pairs, width, rows), jnp.bfloat16),
        jax.ShapeDtypeStruct((pairs, width, rows), jnp.float32),
        jax.ShapeDtypeStruct((pairs, heads, rows), jnp.float32),
        jax.ShapeDtypeStruct((pairs, heads, rows), jnp.float32),
    ]


def rubric_attention(first, some, query, key, value, state, after):
    pairs, rows, width = query.shape
    steps = key.shape[2] // HD
    step_width = width // steps
    heads = width // HD
    count = key.shape[1]

    def spec(size):
        return pl.BlockSpec((1, size, rows), lambda p, g: (first + p, g, 0))

    def across(size):
        return pl.BlockSpec((1, rows, size), lambda p, g: (first + p, 0, g))

    return pl.pallas_call(
        rubric_kernel,
        grid=(some, steps),
        in_specs=[across(step_width), across(HD), across(HD)] + [ANY] * (1 + len(state)),
        out_specs=[spec(step_width), spec(step_width), spec(heads // steps), spec(heads // steps)],
        out_shape=state_shapes(pairs, rows, width),
        input_output_aliases={4 + i: i for i in range(len(state))},
        compiler_params=params("arbitrary", "arbitrary"),
        cost_estimate=hint(
            3 * some * heads * rows * count * HD,
            some * rows * width * 8,
            some * heads * rows * count,
        ),
        name="rubric_attention",
    )(query, key, value, after, *state)


def response_kernel(shift, plan_ref, qt_ref, kv_ref, acc_ref, peak_ref, sum_ref, *refs):
    acc_out, peak_out, sum_out, out_ref = refs[-4:]
    heads = qt_ref.shape[1] // HD
    count = kv_ref.shape[0] // 2
    length = plan_ref[shift * FIELDS + 2]
    wanted = plan_ref[shift * FIELDS + 3] == 1
    completes = plan_ref[shift * FIELDS + 4] == 1

    @pl.when(wanted)
    def _():
        live_rows = lax.broadcasted_iota(jnp.int32, (count, HD), 0) < length
        live_columns = lax.broadcasted_iota(jnp.int32, (HD + SUM_ROWS, count), 1) < length
        block = kv_ref[:count, :].astype(jnp.float32)
        keys = jnp.where(live_rows, block, block[0:1]).astype(jnp.bfloat16)
        values = jnp.concatenate(
            [kv_ref[count:, :].astype(jnp.float32).T, jnp.ones((SUM_ROWS, count), jnp.float32)],
            axis=0,
        )
        values = jnp.where(live_columns, values, 0.0).astype(jnp.bfloat16)
        later = times(keys, qt_ref[0, head_rows(0), :])
        for h in range(heads):
            s = later
            if h + 1 < heads:
                later = times(keys, qt_ref[0, head_rows(h + 1), :])
            old_peak = peak_ref[0, h : h + 1, :]
            peak = jnp.maximum(old_peak, top_of(s))
            fade = jnp.exp2((old_peak - peak) * SCALE)
            pv = times(values, softmax_part(s, peak))
            acc_out[0, head_rows(h), :] = acc_ref[0, head_rows(h), :] * fade + pv[:HD]
            peak_out[0, h : h + 1, :] = peak
            sum_out[0, h : h + 1, :] = sum_ref[0, h : h + 1, :] * fade + pv[HD : HD + 1]

    @pl.when(jnp.logical_not(wanted))
    def _():
        acc_out[...] = acc_ref[...]
        peak_out[...] = peak_ref[...]
        sum_out[...] = sum_ref[...]

    @pl.when(completes | jnp.logical_not(wanted))
    def _():
        for h in range(heads):
            share = acc_out[0, head_rows(h), :] * (1.0 / sum_out[0, h : h + 1, :])
            out_ref[0, :, head_rows(h)] = share.astype(out_ref.dtype).T


def response_attention(shift, plan, kv, state, out):
    pairs, width, rows = state[0].shape
    heads = width // HD
    steps = kv.shape[1] // HD
    step_width = width // steps
    count = kv.shape[0] // 2
    pair_at = shift * FIELDS + 1

    def spec(size):
        return pl.BlockSpec((1, size, rows), lambda g, plan: (plan[pair_at], g, 0))

    state_specs = [spec(step_width), spec(heads // steps), spec(heads // steps)]
    operands = [plan, state[0], kv, *state[1:]]
    in_specs = [
        spec(step_width),
        pl.BlockSpec((2 * count, HD), lambda g, plan: (0, g)),
        *state_specs,
    ]
    aliases = {3: 0, 4: 1, 5: 2}
    if out is not None:
        aliases[len(operands)] = 3
        operands.append(out)
        in_specs.append(ANY)
    results = pl.pallas_call(
        functools.partial(response_kernel, shift),
        grid_spec=pltpu.PrefetchScalarGridSpec(
            num_scalar_prefetch=1,
            grid=(steps,),
            in_specs=in_specs,
            out_specs=state_specs
            + [pl.BlockSpec((1, rows, step_width), lambda g, plan: (plan[pair_at], 0, g))],
        ),
        out_shape=state_shapes(pairs, rows, width)[1:]
        + [jax.ShapeDtypeStruct((pairs, rows, width), jnp.bfloat16)],
        input_output_aliases=aliases,
        compiler_params=params("arbitrary"),
        cost_estimate=hint(
            4 * heads * rows * count * HD, rows * width * 12, heads * rows * count
        ),
        name="response_attention",
    )(*operands)
    return [state[0], *results[:3]], results[3]


def local(
    rubric_query,
    rubric_key,
    rubric_value,
    response_states,
    key_weight,
    value_weight,
    owner_slot,
    response_length,
    pair_table,
):
    groups = lax.axis_size("dp")
    stored, length, depth = response_states.shape
    pairs = rubric_query.shape[0]
    tensor = lax.axis_size("tensor")
    width = key_weight.shape[1] // tensor
    me = lax.axis_index("dp").astype(jnp.int32)
    own_half = lax.axis_index("tensor").astype(jnp.int32)
    other_half = 1 - own_half
    rows = response_states.reshape(stored * length, depth)
    swap = [(0, 1), (1, 0)]
    order = arrival_order(groups)
    place = jnp.array([0] + [1 + order.index(s) for s in range(1, groups)], jnp.int32)
    tables = [owner_slot, response_length, pair_table.T, place]

    other, plan = project_and_plan(
        rows, key_weight, value_weight, other_half, width, me, tables, groups, stored
    )
    received = lax.ppermute(other, "tensor", swap)
    own_keys, own_values = (
        times(rows, lax.dynamic_slice_in_dim(weight, own_half * width, width, 1))
        for weight in (key_weight, value_weight)
    )
    blocks = finish(plan, own_keys, own_values, received, groups, length, "finish")
    arrived = {0: blocks[0]}

    def send(shifts, *after):
        for shift in shifts:
            block = lax.optimization_barrier((blocks[shift], *after))[0]
            arrived[shift] = lax.ppermute(block, "dp", [(g, g ^ shift) for g in range(groups)])

    send(order[:2])
    half = pairs // 2
    state = rubric_attention(
        0, half, rubric_query, rubric_key, rubric_value, (), blocks[0]
    )
    send(order[2:4], state[2])
    state = rubric_attention(
        half, pairs - half, rubric_query, rubric_key, rubric_value, state, arrived[order[1]]
    )
    state, out = response_attention(0, plan, blocks[0], state, None)
    for at in range(0, len(order), 2):
        send(order[at + 4 : at + 6], arrived[order[at]], state[2])
        for shift in order[at : at + 2]:
            state, out = response_attention(shift, plan, arrived[shift], state, out)
    return out


def solution(mesh):
    return jax.shard_map(
        local,
        mesh=mesh,
        in_specs=(
            P(("rep", "dp"), None, "tensor"),
            P(("rep", "dp"), None, "tensor"),
            P(("rep", "dp"), None, "tensor"),
            P(("rep", "dp"), None, "tensor"),
            P("tensor", None),
            P("tensor", None),
            P("rep"),
            P("rep"),
            P("rep", None),
        ),
        out_specs=P(("rep", "dp"), None, "tensor"),
        check_vma=False,
    )
```

```python
import functools
import math

import jax
import jax.numpy as jnp
from jax import lax
from jax.experimental import pallas as pl
from jax.experimental.pallas import tpu as pltpu
from jax.sharding import PartitionSpec as P

HD = 128
SCALE = HD ** (-0.5) * math.log2(math.e)
MIB = 1024 * 1024
FIELDS = 5
SUM_ROWS = 16
NEVER = -1e30
NEAR = 100.0
ANY = pl.BlockSpec(memory_space=pl.ANY)
SMEM = pl.BlockSpec(memory_space=pltpu.SMEM)
WHOLE = pl.BlockSpec(memory_space=pltpu.VMEM)


def params(*semantics, vmem=24):
    return pltpu.CompilerParams(
        dimension_semantics=semantics or None, vmem_limit_bytes=vmem * MIB
    )


def hint(flops, bytes_accessed, transcendentals):
    return pl.CostEstimate(
        flops=flops, bytes_accessed=bytes_accessed, transcendentals=transcendentals
    )


def arrival_order(groups):
    far = list(range(groups - 1, groups // 2 - 1, -1))
    near = list(range(groups // 2 - 1, 0, -1))
    order = []
    for at in range(len(far)):
        order += far[at : at + 1] + near[at : at + 1]
    return order


def write_plan(groups, stored, me, owner_ref, length_ref, table_ref, place_ref, plan_ref):
    pairs = table_ref.shape[1] // groups
    bits = stored.bit_length() - 1

    def slot_of(group, j):
        response = table_ref[j % 2, group * pairs + j // 2]
        slot = owner_ref[response]
        return response, lax.shift_right_logical(slot, bits), slot & (stored - 1)

    for shift in range(groups):
        plan_ref[shift * FIELDS + 3] = 0
        plan_ref[shift * FIELDS + 1] = 0
        row = jnp.int32(0)
        for j in range(2 * pairs):
            _, source, slot_row = slot_of(me ^ shift, j)
            row = jnp.where(source == me, slot_row, row)
        plan_ref[shift * FIELDS] = row
    sources = [slot_of(me, j) for j in range(2 * pairs)]
    for j, (response, source, _) in enumerate(sources):
        shift = source ^ me
        later = place_ref[shift] > place_ref[sources[j ^ 1][1] ^ me]
        plan_ref[shift * FIELDS + 1] = jnp.int32(j // 2)
        plan_ref[shift * FIELDS + 2] = length_ref[response]
        plan_ref[shift * FIELDS + 3] = jnp.int32(1)
        plan_ref[shift * FIELDS + 4] = later.astype(jnp.int32)


def plan_kernel(groups, stored, me_ref, owner_ref, length_ref, table_ref, place_ref, plan_ref):
    write_plan(groups, stored, me_ref[0], owner_ref, length_ref, table_ref, place_ref, plan_ref)


def make_plan(me, tables, groups, stored):
    return pl.pallas_call(
        functools.partial(plan_kernel, groups, stored),
        out_shape=jax.ShapeDtypeStruct((groups * FIELDS,), jnp.int32),
        in_specs=[SMEM] * 5,
        out_specs=SMEM,
        name="plan",
    )(me[None], *tables)


def finish_kernel(length, plan_ref, own_keys_ref, own_values_ref, keys_ref, values_ref, *out_refs):
    for shift, out_ref in enumerate(out_refs):
        start = pl.multiple_of(plan_ref[shift * FIELDS] * length, length)
        rows = pl.ds(start, length)
        for at, (own_ref, other_ref) in enumerate(
            ((own_keys_ref, keys_ref), (own_values_ref, values_ref))
        ):
            total = own_ref[rows, :] + other_ref[rows, :]
            out_ref[at * length : (at + 1) * length, :] = total.astype(out_ref.dtype)


def finish(plan, own_keys, own_values, other_keys, other_values, groups, length):
    total, width = own_keys.shape
    return pl.pallas_call(
        functools.partial(finish_kernel, length),
        out_shape=[jax.ShapeDtypeStruct((2 * length, width), jnp.bfloat16)] * groups,
        in_specs=[SMEM] + [WHOLE] * 4,
        out_specs=[WHOLE] * groups,
        compiler_params=params(),
        cost_estimate=hint(
            2 * groups * length * width,
            16 * total * width + 4 * groups * length * width,
            0,
        ),
        name="finish",
    )(plan, own_keys, own_values, other_keys, other_values)


def times(a, b):
    return jnp.dot(a, b, preferred_element_type=jnp.float32)


def head_rows(h):
    return slice(h * HD, (h + 1) * HD)


def softmax_part(s, peak):
    return jnp.exp2(s * SCALE - peak * SCALE).astype(jnp.bfloat16)


def top_of(s):
    return jnp.max(s, axis=0, keepdims=True)


def length_of(x, axis):
    return jnp.sqrt(jnp.sum(x * x, axis=axis, keepdims=True))


def rubric_kernel(q_ref, k_ref, v_ref, *refs):
    qt_ref, reach_ref, acc_ref, peak_ref, sum_ref = refs[-5:]
    heads = qt_ref.shape[1] // HD
    half = k_ref.shape[1] // 2
    keys = k_ref[0]
    values = jnp.concatenate(
        [v_ref[0].T, jnp.ones((SUM_ROWS, 2 * half), jnp.bfloat16)], axis=0
    )
    shape = (half, half)
    causal = lax.broadcasted_iota(jnp.int32, shape, 0) <= lax.broadcasted_iota(jnp.int32, shape, 1)
    for h in range(heads):
        turned = q_ref[0, :, head_rows(h)].T
        qt_ref[0, head_rows(h), :] = turned
        reach_ref[0, h : h + 1, :] = length_of(turned.astype(jnp.float32), 0) * SCALE

    def scores(h):
        turned = qt_ref[0, head_rows(h), :]
        return times(keys[:half], turned), times(keys[half:], turned[:, half:])

    def weigh(h, first, last, early_peak, late_peak):
        early = jnp.where(causal, first[:, :half], NEVER)
        last = jnp.where(causal, last, NEVER)
        weights = jnp.concatenate(
            [softmax_part(early, early_peak), softmax_part(first[:, half:], late_peak)], axis=1
        )
        pv = times(values[:, :half], weights)
        more = times(values[:, half:], softmax_part(last, late_peak))
        acc_ref[0, head_rows(h), :half] = pv[:HD, :half]
        acc_ref[0, head_rows(h), half:] = pv[:HD, half:] + more[:HD]
        peak_ref[0, h : h + 1, :half] = early_peak
        peak_ref[0, h : h + 1, half:] = late_peak
        sum_ref[0, h : h + 1, :half] = pv[HD : HD + 1, :half]
        sum_ref[0, h : h + 1, half:] = pv[HD : HD + 1, half:] + more[HD : HD + 1]

    longest = jnp.max(length_of(keys.astype(jnp.float32), 1))
    near = 2.0 * jnp.max(reach_ref[...]) * longest < NEAR

    @pl.when(near)
    def _():
        later = scores(0)
        for h in range(heads):
            first, last = later
            if h + 1 < heads:
                later = scores(h + 1)
            weigh(h, first, last, first[0:1, :half], first[0:1, half:])

    @pl.when(jnp.logical_not(near))
    def _():
        for h in range(heads):
            first, last = scores(h)
            early_peak = top_of(jnp.where(causal, first[:, :half], NEVER))
            late_peak = jnp.maximum(
                top_of(first[:, half:]), top_of(jnp.where(causal, last, NEVER))
            )
            weigh(h, first, last, early_peak, late_peak)


def state_shapes(pairs, rows, width):
    heads = width // HD
    return [
        jax.ShapeDtypeStruct((pairs, width, rows), jnp.bfloat16),
        jax.ShapeDtypeStruct((pairs, heads, rows), jnp.float32),
        jax.ShapeDtypeStruct((pairs, width, rows), jnp.float32),
        jax.ShapeDtypeStruct((pairs, heads, rows), jnp.float32),
        jax.ShapeDtypeStruct((pairs, heads, rows), jnp.float32),
    ]


def rubric_attention(first, some, query, key, value, state, after):
    pairs, rows, width = query.shape
    steps = key.shape[2] // HD
    step_width = width // steps
    heads = width // HD
    count = key.shape[1]

    def spec(size):
        return pl.BlockSpec((1, size, rows), lambda p, g: (first + p, g, 0))

    small = spec(heads // steps)

    def across(size):
        return pl.BlockSpec((1, rows, size), lambda p, g: (first + p, 0, g))

    return pl.pallas_call(
        rubric_kernel,
        grid=(some, steps),
        in_specs=[across(step_width), across(HD), across(HD)] + [ANY] * (1 + len(state)),
        out_specs=[spec(step_width), small, spec(step_width), small, small],
        out_shape=state_shapes(pairs, rows, width),
        input_output_aliases={4 + i: i for i in range(len(state))},
        compiler_params=params("arbitrary", "arbitrary"),
        cost_estimate=hint(
            3 * some * heads * rows * count * HD,
            some * rows * width * 8,
            some * heads * rows * count,
        ),
        name="rubric_attention",
    )(query, key, value, after, *state)


def response_kernel(
    shift, plan_ref, qt_ref, reach_ref, kv_ref, acc_ref, peak_ref, sum_ref, *refs
):
    acc_out, peak_out, sum_out, out_ref = refs[-4:]
    heads = qt_ref.shape[1] // HD
    count = kv_ref.shape[0] // 2
    length = plan_ref[shift * FIELDS + 2]
    wanted = plan_ref[shift * FIELDS + 3] == 1
    completes = plan_ref[shift * FIELDS + 4] == 1

    @pl.when(wanted)
    def _():
        live_rows = lax.broadcasted_iota(jnp.int32, (count, HD), 0) < length
        live_columns = lax.broadcasted_iota(jnp.int32, (HD + SUM_ROWS, count), 1) < length
        block = kv_ref[:count, :].astype(jnp.float32)
        keys = jnp.where(live_rows, block, block[0:1]).astype(jnp.bfloat16)
        values = jnp.concatenate(
            [kv_ref[count:, :].astype(jnp.float32).T, jnp.ones((SUM_ROWS, count), jnp.float32)],
            axis=0,
        )
        values = jnp.where(live_columns, values, 0.0).astype(jnp.bfloat16)

        def scores(h):
            return times(keys, qt_ref[0, head_rows(h), :])

        longest = jnp.max(length_of(keys.astype(jnp.float32), 1))
        near = jnp.max(reach_ref[...] * longest - peak_ref[...] * SCALE) < NEAR

        @pl.when(near)
        def _():
            later = scores(0)
            for h in range(heads):
                s = later
                if h + 1 < heads:
                    later = scores(h + 1)
                pv = times(values, softmax_part(s, peak_ref[0, h : h + 1, :]))
                acc_out[0, head_rows(h), :] = acc_ref[0, head_rows(h), :] + pv[:HD]
                sum_out[0, h : h + 1, :] = sum_ref[0, h : h + 1, :] + pv[HD : HD + 1]
            peak_out[...] = peak_ref[...]

        @pl.when(jnp.logical_not(near))
        def _():
            for h in range(heads):
                s = scores(h)
                old_peak = peak_ref[0, h : h + 1, :]
                peak = jnp.maximum(old_peak, top_of(s))
                fade = jnp.exp2((old_peak - peak) * SCALE)
                pv = times(values, softmax_part(s, peak))
                acc_out[0, head_rows(h), :] = acc_ref[0, head_rows(h), :] * fade + pv[:HD]
                peak_out[0, h : h + 1, :] = peak
                sum_out[0, h : h + 1, :] = sum_ref[0, h : h + 1, :] * fade + pv[HD : HD + 1]

    @pl.when(jnp.logical_not(wanted))
    def _():
        acc_out[...] = acc_ref[...]
        peak_out[...] = peak_ref[...]
        sum_out[...] = sum_ref[...]

    @pl.when(completes | jnp.logical_not(wanted))
    def _():
        for h in range(heads):
            share = acc_out[0, head_rows(h), :] * (1.0 / sum_out[0, h : h + 1, :])
            out_ref[0, :, head_rows(h)] = share.astype(out_ref.dtype).T


def response_attention(shift, plan, kv, state, out):
    pairs, width, rows = state[0].shape
    heads = width // HD
    steps = kv.shape[1] // HD
    step_width = width // steps
    count = kv.shape[0] // 2
    pair_at = shift * FIELDS + 1

    def spec(size):
        return pl.BlockSpec((1, size, rows), lambda g, plan: (plan[pair_at], g, 0))

    small = spec(heads // steps)
    state_specs = [spec(step_width), small, small]
    operands = [plan, *state[:2], kv, *state[2:]]
    in_specs = [
        spec(step_width),
        small,
        pl.BlockSpec((2 * count, HD), lambda g, plan: (0, g)),
        *state_specs,
    ]
    aliases = {4: 0, 5: 1, 6: 2}
    if out is not None:
        aliases[len(operands)] = 3
        operands.append(out)
        in_specs.append(ANY)
    results = pl.pallas_call(
        functools.partial(response_kernel, shift),
        grid_spec=pltpu.PrefetchScalarGridSpec(
            num_scalar_prefetch=1,
            grid=(steps,),
            in_specs=in_specs,
            out_specs=state_specs
            + [pl.BlockSpec((1, rows, step_width), lambda g, plan: (plan[pair_at], 0, g))],
        ),
        out_shape=state_shapes(pairs, rows, width)[2:]
        + [jax.ShapeDtypeStruct((pairs, rows, width), jnp.bfloat16)],
        input_output_aliases=aliases,
        compiler_params=params("arbitrary"),
        cost_estimate=hint(
            4 * heads * rows * count * HD, rows * width * 12, heads * rows * count
        ),
        name="response_attention",
    )(*operands)
    return [*state[:2], *results[:3]], results[3]


def local(
    rubric_query,
    rubric_key,
    rubric_value,
    response_states,
    key_weight,
    value_weight,
    owner_slot,
    response_length,
    pair_table,
):
    groups = lax.axis_size("dp")
    stored, length, depth = response_states.shape
    pairs = rubric_query.shape[0]
    tensor = lax.axis_size("tensor")
    width = key_weight.shape[1] // tensor
    me = lax.axis_index("dp").astype(jnp.int32)
    own_half = lax.axis_index("tensor").astype(jnp.int32)
    other_half = 1 - own_half
    rows = response_states.reshape(stored * length, depth)
    swap = [(0, 1), (1, 0)]
    order = arrival_order(groups)
    place = jnp.array([0] + [1 + order.index(s) for s in range(1, groups)], jnp.int32)
    tables = [owner_slot, response_length, pair_table.T, place]

    plan = make_plan(me, tables, groups, stored)

    def project(half):
        return [
            times(rows, lax.dynamic_slice_in_dim(weight, half * width, width, 1))
            for weight in (key_weight, value_weight)
        ]

    received = [lax.ppermute(part, "tensor", swap) for part in project(other_half)]
    blocks = finish(plan, *project(own_half), *received, groups, length)
    arrived = {0: blocks[0]}

    def send(shifts, *after):
        for shift in shifts:
            block = lax.optimization_barrier((blocks[shift], *after))[0]
            arrived[shift] = lax.ppermute(block, "dp", [(g, g ^ shift) for g in range(groups)])

    send(order[:2])
    half = pairs // 2
    state = rubric_attention(
        0, half, rubric_query, rubric_key, rubric_value, (), blocks[0]
    )
    send(order[2:4], state[3])
    state = rubric_attention(
        half, pairs - half, rubric_query, rubric_key, rubric_value, state, arrived[order[1]]
    )
    state, out = response_attention(0, plan, blocks[0], state, None)
    for at in range(0, len(order), 2):
        send(order[at + 4 : at + 6], arrived[order[at]], state[3])
        for shift in order[at : at + 2]:
            state, out = response_attention(shift, plan, arrived[shift], state, out)
    return out


def solution(mesh):
    return jax.shard_map(
        local,
        mesh=mesh,
        in_specs=(
            P(("rep", "dp"), None, "tensor"),
            P(("rep", "dp"), None, "tensor"),
            P(("rep", "dp"), None, "tensor"),
            P(("rep", "dp"), None, "tensor"),
            P("tensor", None),
            P("tensor", None),
            P("rep"),
            P("rep"),
            P("rep", None),
        ),
        out_specs=P(("rep", "dp"), None, "tensor"),
        check_vma=False,
    )
```

```python
import functools
import math

import jax
import jax.numpy as jnp
from jax import lax
from jax.experimental import pallas as pl
from jax.experimental.pallas import tpu as pltpu
from jax.sharding import PartitionSpec as P

HD = 128
SCALE = HD ** (-0.5) * math.log2(math.e)
MIB = 1024 * 1024
FIELDS = 5
NEVER = -1e30
NEAR = 100.0
FAR = 1e30
TOGETHER = 2
SHIFT_LANE = HD + HD // 2
ANY = pl.BlockSpec(memory_space=pl.ANY)
SMEM = pl.BlockSpec(memory_space=pltpu.SMEM)
WHOLE = pl.BlockSpec(memory_space=pltpu.VMEM)


def params(*semantics, vmem=12):
    return pltpu.CompilerParams(
        dimension_semantics=semantics or None, vmem_limit_bytes=vmem * MIB
    )


def hint(flops, bytes_accessed, transcendentals):
    return pl.CostEstimate(
        flops=flops, bytes_accessed=bytes_accessed, transcendentals=transcendentals
    )


def arrival_order(groups):
    far = list(range(groups - 1, groups // 2 - 1, -1))
    near = list(range(groups // 2 - 1, 0, -1))
    order = []
    for at in range(len(far)):
        order += far[at : at + 1] + near[at : at + 1]
    return order


def write_plan(groups, stored, me, owner_ref, length_ref, table_ref, place_ref, plan_ref):
    pairs = table_ref.shape[1] // groups
    bits = stored.bit_length() - 1

    def slot_of(group, j):
        response = table_ref[j % 2, group * pairs + j // 2]
        slot = owner_ref[response]
        return response, lax.shift_right_logical(slot, bits), slot & (stored - 1)

    for shift in range(groups):
        plan_ref[shift * FIELDS + 3] = 0
        plan_ref[shift * FIELDS + 1] = 0
        row = jnp.int32(0)
        for j in range(2 * pairs):
            _, source, slot_row = slot_of(me ^ shift, j)
            row = jnp.where(source == me, slot_row, row)
        plan_ref[shift * FIELDS] = row
    sources = [slot_of(me, j) for j in range(2 * pairs)]
    for j, (response, source, _) in enumerate(sources):
        shift = source ^ me
        later = place_ref[shift] > place_ref[sources[j ^ 1][1] ^ me]
        plan_ref[shift * FIELDS + 1] = jnp.int32(j // 2)
        plan_ref[shift * FIELDS + 2] = length_ref[response]
        plan_ref[shift * FIELDS + 3] = jnp.int32(1)
        plan_ref[shift * FIELDS + 4] = later.astype(jnp.int32)


def plan_kernel(groups, stored, me_ref, owner_ref, length_ref, table_ref, place_ref, plan_ref):
    write_plan(groups, stored, me_ref[0], owner_ref, length_ref, table_ref, place_ref, plan_ref)


def make_plan(me, tables, groups, stored):
    return pl.pallas_call(
        functools.partial(plan_kernel, groups, stored),
        out_shape=jax.ShapeDtypeStruct((groups * FIELDS,), jnp.int32),
        in_specs=[SMEM] * 5,
        out_specs=SMEM,
        name="plan",
    )(me[None], *tables)


def finish_kernel(length, plan_ref, half_ref, own_keys_ref, own_values_ref, keys_ref, values_ref, *out_refs):
    width = keys_ref.shape[1]
    own_columns = pl.ds(pl.multiple_of(half_ref[0] * width, width), width)
    for shift, out_ref in enumerate(out_refs):
        start = pl.multiple_of(plan_ref[shift * FIELDS] * length, length)
        rows = pl.ds(start, length)
        for at, (own_ref, other_ref) in enumerate(
            ((own_keys_ref, keys_ref), (own_values_ref, values_ref))
        ):
            total = own_ref[rows, own_columns] + other_ref[rows, :]
            out_ref[at * length : (at + 1) * length, :] = total.astype(out_ref.dtype)


def finish(plan, half, own_keys, own_values, other_keys, other_values, groups, length):
    total, width = other_keys.shape
    return pl.pallas_call(
        functools.partial(finish_kernel, length),
        out_shape=[jax.ShapeDtypeStruct((2 * length, width), jnp.bfloat16)] * groups,
        in_specs=[SMEM] * 2 + [WHOLE] * 4,
        out_specs=[WHOLE] * groups,
        compiler_params=params(),
        cost_estimate=hint(
            2 * groups * length * width, 16 * total * width + 4 * groups * length * width, 0
        ),
        name="finish",
    )(plan, half[None], own_keys, own_values, other_keys, other_values)


def times(a, b):
    return jnp.dot(a, b, preferred_element_type=jnp.float32)


def head_columns(h):
    return slice(h * HD, (h + 1) * HD)


def queries_of(q_ref, first, some):
    return jnp.concatenate([q_ref[0, :, head_columns(h)] for h in range(first, first + some)])


def with_ones(values):
    lane = lax.broadcasted_iota(jnp.int32, values.shape, 1)
    ones = jnp.where(lane < HD // 2, 1.0, 0.0).astype(values.dtype)
    return jnp.concatenate([values, ones], axis=1)


def longest_of(keys):
    keys = keys.astype(jnp.float32)
    return jnp.sqrt(jnp.max(jnp.sum(keys * keys, axis=1, keepdims=True)))


def in_range(reach, keys):
    return jnp.max(reach) * longest_of(keys) < NEAR


def keep_shift(state, shift):
    lane = lax.broadcasted_iota(jnp.int32, state.shape, 1)
    return jnp.where(lane >= SHIFT_LANE, shift, state)


def rubric_kernel(q_ref, k_ref, v_ref, *refs):
    reach_ref, state_ref = refs[-2:]
    rows = q_ref.shape[1]
    heads = q_ref.shape[2] // HD
    keys = k_ref[0]
    turned = keys.T
    values = with_ones(v_ref[0])
    shape = (rows, keys.shape[0])
    causal = lax.broadcasted_iota(jnp.int32, shape, 0) >= lax.broadcasted_iota(jnp.int32, shape, 1)
    allowed = jnp.where(causal, 1.0, 0.0).astype(jnp.bfloat16)
    allowed = jnp.concatenate([allowed] * TOGETHER)
    ones = jnp.ones((HD, HD), jnp.bfloat16)
    reach = jnp.zeros((rows, HD), jnp.float32)
    for h in range(heads):
        q = q_ref[0, :, head_columns(h)]
        reach = jnp.maximum(reach, times(q * q, ones))
    reach = jnp.max(reach.reshape(rows // 8, 8, HD), axis=0)
    reach = jnp.sqrt(reach) * (SCALE * 1.01)
    near = in_range(reach, keys)
    reach_ref[0, 0] = jnp.where(near, reach, FAR)

    @pl.when(near)
    def _():
        later = times(queries_of(q_ref, 0, TOGETHER), turned)
        for h in range(0, heads, TOGETHER):
            s = later
            if h + TOGETHER < heads:
                later = times(queries_of(q_ref, h + TOGETHER, TOGETHER), turned)
            weights = jnp.exp2(s * SCALE).astype(jnp.bfloat16) * allowed
            state_ref[0, 0, h * rows : (h + TOGETHER) * rows, :] = times(weights, values)

    @pl.when(jnp.logical_not(near))
    def _():
        for h in range(heads):
            s = jnp.where(causal, times(q_ref[0, :, head_columns(h)], turned), NEVER)
            peak = jnp.max(s, axis=1, keepdims=True)
            weights = jnp.exp2((s - peak) * SCALE).astype(jnp.bfloat16)
            state_ref[0, 0, h * rows : (h + 1) * rows, :] = keep_shift(times(weights, values), peak)


def state_shapes(pairs, kv_heads, stacked):
    return [
        jax.ShapeDtypeStruct((pairs, kv_heads, 8, HD), jnp.float32),
        jax.ShapeDtypeStruct((pairs, kv_heads, stacked, 2 * HD), jnp.float32),
    ]


def rubric_attention(first, some, query, key, value, state, after):
    pairs, rows, width = query.shape
    steps = key.shape[2] // HD
    step_width = width // steps
    stacked = step_width // HD * rows
    count = key.shape[1]

    def across(size):
        return pl.BlockSpec((1, rows, size), lambda p, g: (first + p, 0, g))

    return pl.pallas_call(
        rubric_kernel,
        grid=(some, steps),
        in_specs=[across(step_width), across(HD), across(HD)] + [ANY] * (1 + len(state)),
        out_specs=[
            pl.BlockSpec((1, 1, 8, HD), lambda p, g: (first + p, g, 0, 0)),
            pl.BlockSpec((1, 1, stacked, 2 * HD), lambda p, g: (first + p, g, 0, 0)),
        ],
        out_shape=state_shapes(pairs, steps, stacked),
        input_output_aliases={4 + i: i for i in range(len(state))},
        compiler_params=params("arbitrary", "arbitrary"),
        cost_estimate=hint(
            6 * some * width * rows * count,
            some * rows * width * 8,
            some * width // HD * rows * count,
        ),
        name="rubric_attention",
    )(query, key, value, after, *state)


def response_kernel(shift, plan_ref, q_ref, kv_ref, reach_ref, state_ref, *refs):
    reach_out, state_out, out_ref = refs[-3:]
    rows = q_ref.shape[1]
    heads = q_ref.shape[2] // HD
    count = kv_ref.shape[0] // 2
    length = plan_ref[shift * FIELDS + 2]
    wanted = plan_ref[shift * FIELDS + 3] == 1
    completes = plan_ref[shift * FIELDS + 4] == 1

    def stack(h, some):
        return slice(h * rows, (h + some) * rows)

    @pl.when(wanted)
    def _():
        turned = kv_ref[:count, :].T
        values = with_ones(kv_ref[count:, :].astype(jnp.float32))
        live = lax.broadcasted_iota(jnp.int32, values.shape, 0) < length
        values = jnp.where(live, values, 0.0).astype(jnp.bfloat16)
        near = in_range(reach_ref[...], kv_ref[:count, :])

        @pl.when(near)
        def _():
            reach_out[...] = reach_ref[...]
            later = times(queries_of(q_ref, 0, TOGETHER), turned)
            for h in range(0, heads, TOGETHER):
                s = later
                if h + TOGETHER < heads:
                    later = times(queries_of(q_ref, h + TOGETHER, TOGETHER), turned)
                weights = jnp.exp2(s * SCALE).astype(jnp.bfloat16)
                at = stack(h, TOGETHER)
                state_out[0, 0, at, :] = state_ref[0, 0, at, :] + times(weights, values)

        @pl.when(jnp.logical_not(near))
        def _():
            reach_out[...] = jnp.full(reach_out.shape, FAR, jnp.float32)
            columns = lax.broadcasted_iota(jnp.int32, (rows, count), 1)
            for h in range(heads):
                s = times(q_ref[0, :, head_columns(h)], turned)
                s = jnp.where(columns < length, s, NEVER)
                old = state_ref[0, 0, stack(h, 1), :]
                old_peak = old[:, SHIFT_LANE : SHIFT_LANE + 1]
                peak = jnp.maximum(old_peak, jnp.max(s, axis=1, keepdims=True))
                weights = jnp.exp2((s - peak) * SCALE).astype(jnp.bfloat16)
                new = old * jnp.exp2((old_peak - peak) * SCALE) + times(weights, values)
                state_out[0, 0, stack(h, 1), :] = keep_shift(new, peak)

    @pl.when(jnp.logical_not(wanted))
    def _():
        reach_out[...] = reach_ref[...]
        state_out[...] = state_ref[...]

    @pl.when(completes | jnp.logical_not(wanted))
    def _():
        for h in range(heads):
            state = state_out[0, 0, stack(h, 1), :]
            share = state[:, :HD] / state[:, HD : HD + 1]
            out_ref[0, :, head_columns(h)] = share.astype(out_ref.dtype)


def response_attention(shift, plan, query, kv, state, out):
    pairs, rows, width = query.shape
    steps = kv.shape[1] // HD
    step_width = width // steps
    stacked = step_width // HD * rows
    count = kv.shape[0] // 2
    pair_at = shift * FIELDS + 1
    across = pl.BlockSpec((1, rows, step_width), lambda g, plan: (plan[pair_at], 0, g))
    state_specs = [
        pl.BlockSpec((1, 1, 8, HD), lambda g, plan: (plan[pair_at], g, 0, 0)),
        pl.BlockSpec((1, 1, stacked, 2 * HD), lambda g, plan: (plan[pair_at], g, 0, 0)),
    ]
    operands = [plan, query, kv, *state]
    in_specs = [across, pl.BlockSpec((2 * count, HD), lambda g, plan: (0, g)), *state_specs]
    aliases = {3: 0, 4: 1}
    if out is not None:
        aliases[len(operands)] = 2
        operands.append(out)
        in_specs.append(ANY)
    *state, out = pl.pallas_call(
        functools.partial(response_kernel, shift),
        grid_spec=pltpu.PrefetchScalarGridSpec(
            num_scalar_prefetch=1,
            grid=(steps,),
            in_specs=in_specs,
            out_specs=state_specs + [across],
        ),
        out_shape=state_shapes(pairs, steps, stacked)
        + [jax.ShapeDtypeStruct(query.shape, jnp.bfloat16)],
        input_output_aliases=aliases,
        compiler_params=params("arbitrary"),
        cost_estimate=hint(
            6 * width * rows * count, rows * width * 12, width // HD * rows * count
        ),
        name="response_attention",
    )(*operands)
    return state, out


def local(
    rubric_query,
    rubric_key,
    rubric_value,
    response_states,
    key_weight,
    value_weight,
    owner_slot,
    response_length,
    pair_table,
):
    groups = lax.axis_size("dp")
    stored, length, depth = response_states.shape
    pairs = rubric_query.shape[0]
    tensor = lax.axis_size("tensor")
    width = key_weight.shape[1] // tensor
    me = lax.axis_index("dp").astype(jnp.int32)
    own_half = lax.axis_index("tensor").astype(jnp.int32)
    other_half = 1 - own_half
    rows = response_states.reshape(stored * length, depth)
    swap = [(0, 1), (1, 0)]
    order = arrival_order(groups)
    place = jnp.array([0] + [1 + order.index(s) for s in range(1, groups)], jnp.int32)
    tables = [owner_slot, response_length, pair_table.T, place]

    plan = make_plan(me, tables, groups, stored)

    def other_columns(part):
        return lax.dynamic_slice_in_dim(part, other_half * width, width, 1)

    own_keys = times(rows, key_weight)
    keys_in = lax.ppermute(other_columns(own_keys), "tensor", swap)
    own_values = times(rows, value_weight)
    values_out = other_columns(own_values)
    values_in = lax.ppermute(values_out, "tensor", swap)
    first = rubric_attention(0, 1, rubric_query, rubric_key, rubric_value, (), values_out)
    blocks = finish(
        plan,
        own_half,
        own_keys,
        own_values,
        keys_in,
        lax.optimization_barrier((values_in, first[0]))[0],
        groups,
        length,
    )
    arrived = {0: blocks[0]}

    def send(shifts, *after):
        for shift in shifts:
            block = lax.optimization_barrier((blocks[shift], *after))[0]
            arrived[shift] = lax.ppermute(block, "dp", [(g, g ^ shift) for g in range(groups)])

    send(order[:2])
    half = 1 + (pairs - 1) // 2
    state = rubric_attention(
        1, half - 1, rubric_query, rubric_key, rubric_value, first, blocks[0]
    )
    send(order[2:4], state[0])
    state = rubric_attention(
        half, pairs - half, rubric_query, rubric_key, rubric_value, state, arrived[order[1]]
    )
    state, out = response_attention(0, plan, rubric_query, blocks[0], state, None)
    for at in range(0, len(order), 2):
        send(order[at + 4 : at + 6], arrived[order[at]], state[0])
        for shift in order[at : at + 2]:
            state, out = response_attention(
                shift, plan, rubric_query, arrived[shift], state, out
            )
    return out


def solution(mesh):
    return jax.shard_map(
        local,
        mesh=mesh,
        in_specs=(
            P(("rep", "dp"), None, "tensor"),
            P(("rep", "dp"), None, "tensor"),
            P(("rep", "dp"), None, "tensor"),
            P(("rep", "dp"), None, "tensor"),
            P("tensor", None),
            P("tensor", None),
            P("rep"),
            P("rep"),
            P("rep", None),
        ),
        out_specs=P(("rep", "dp"), None, "tensor"),
        check_vma=False,
    )
```

```python
import functools
import math

import jax
import jax.numpy as jnp
from jax import lax
from jax.experimental import pallas as pl
from jax.experimental.pallas import tpu as pltpu
from jax.sharding import PartitionSpec as P

HD = 128
SCALE = HD ** (-0.5) * math.log2(math.e)
MIB = 1024 * 1024
FIELDS = 5
NEVER = -1e30
NEAR = 100.0
FAR = 1e30
TOGETHER = 2
EXTRA_ROWS = 16
SHIFT_ROW = HD + EXTRA_ROWS // 2
ANY = pl.BlockSpec(memory_space=pl.ANY)
SMEM = pl.BlockSpec(memory_space=pltpu.SMEM)
WHOLE = pl.BlockSpec(memory_space=pltpu.VMEM)


def params(*semantics, vmem=12):
    return pltpu.CompilerParams(
        dimension_semantics=semantics or None, vmem_limit_bytes=vmem * MIB
    )


def hint(flops, bytes_accessed, transcendentals):
    return pl.CostEstimate(
        flops=flops, bytes_accessed=bytes_accessed, transcendentals=transcendentals
    )


def arrival_order(groups):
    far = list(range(groups - 1, groups // 2 - 1, -1))
    near = list(range(groups // 2 - 1, 0, -1))
    order = []
    for at in range(len(far)):
        order += far[at : at + 1] + near[at : at + 1]
    return order


def write_plan(groups, stored, me, owner_ref, length_ref, table_ref, place_ref, plan_ref):
    pairs = table_ref.shape[1] // groups
    bits = stored.bit_length() - 1

    def slot_of(group, j):
        response = table_ref[j % 2, group * pairs + j // 2]
        slot = owner_ref[response]
        return response, lax.shift_right_logical(slot, bits), slot & (stored - 1)

    for shift in range(groups):
        plan_ref[shift * FIELDS + 3] = 0
        plan_ref[shift * FIELDS + 1] = 0
        row = jnp.int32(0)
        for j in range(2 * pairs):
            _, source, slot_row = slot_of(me ^ shift, j)
            row = jnp.where(source == me, slot_row, row)
        plan_ref[shift * FIELDS] = row
    sources = [slot_of(me, j) for j in range(2 * pairs)]
    for j, (response, source, _) in enumerate(sources):
        shift = source ^ me
        later = place_ref[shift] > place_ref[sources[j ^ 1][1] ^ me]
        plan_ref[shift * FIELDS + 1] = jnp.int32(j // 2)
        plan_ref[shift * FIELDS + 2] = length_ref[response]
        plan_ref[shift * FIELDS + 3] = jnp.int32(1)
        plan_ref[shift * FIELDS + 4] = later.astype(jnp.int32)


def plan_kernel(groups, stored, me_ref, owner_ref, length_ref, table_ref, place_ref, plan_ref):
    write_plan(groups, stored, me_ref[0], owner_ref, length_ref, table_ref, place_ref, plan_ref)


def make_plan(me, tables, groups, stored):
    return pl.pallas_call(
        functools.partial(plan_kernel, groups, stored),
        out_shape=jax.ShapeDtypeStruct((groups * FIELDS,), jnp.int32),
        in_specs=[SMEM] * 5,
        out_specs=SMEM,
        name="plan",
    )(me[None], *tables)


def finish_kernel(length, plan_ref, half_ref, own_keys_ref, own_values_ref, keys_ref, values_ref, *out_refs):
    width = keys_ref.shape[1]
    own_columns = pl.ds(pl.multiple_of(half_ref[0] * width, width), width)
    for shift, out_ref in enumerate(out_refs):
        start = pl.multiple_of(plan_ref[shift * FIELDS] * length, length)
        rows = pl.ds(start, length)
        for at, (own_ref, other_ref) in enumerate(
            ((own_keys_ref, keys_ref), (own_values_ref, values_ref))
        ):
            total = own_ref[rows, own_columns] + other_ref[rows, :]
            out_ref[at * length : (at + 1) * length, :] = total.astype(out_ref.dtype)


def finish(plan, half, own_keys, own_values, other_keys, other_values, groups, length):
    total, width = other_keys.shape
    return pl.pallas_call(
        functools.partial(finish_kernel, length),
        out_shape=[jax.ShapeDtypeStruct((2 * length, width), jnp.bfloat16)] * groups,
        in_specs=[SMEM] * 2 + [WHOLE] * 4,
        out_specs=[WHOLE] * groups,
        compiler_params=params(),
        cost_estimate=hint(
            2 * groups * length * width, 16 * total * width + 4 * groups * length * width, 0
        ),
        name="finish",
    )(plan, half[None], own_keys, own_values, other_keys, other_values)


def times(a, b):
    return jnp.dot(a, b, preferred_element_type=jnp.float32)


def head_columns(h):
    return slice(h * HD, (h + 1) * HD)


def turned_values(values):
    count = values.shape[0]
    row = lax.broadcasted_iota(jnp.int32, (EXTRA_ROWS, count), 0)
    ones = jnp.where(row < EXTRA_ROWS // 2, 1.0, 0.0)
    return jnp.concatenate([values.astype(jnp.float32).T, ones], axis=0)


def longest_of(keys):
    keys = keys.astype(jnp.float32)
    return jnp.sqrt(jnp.max(jnp.sum(keys * keys, axis=1, keepdims=True)))


def in_range(reach, keys):
    return jnp.max(reach) * longest_of(keys) < NEAR


def keep_shift(state, shift):
    row = lax.broadcasted_iota(jnp.int32, state.shape, 0)
    return jnp.where(row >= SHIFT_ROW, shift, state)


def rubric_kernel(q_ref, k_ref, v_ref, *refs):
    qt_ref, reach_ref, state_ref = refs[-3:]
    rows = q_ref.shape[1]
    heads = q_ref.shape[2] // HD
    keys = k_ref[0]
    values = turned_values(v_ref[0]).astype(jnp.bfloat16)
    shape = (keys.shape[0], rows)
    causal = lax.broadcasted_iota(jnp.int32, shape, 0) <= lax.broadcasted_iota(jnp.int32, shape, 1)
    allowed = jnp.where(causal, 1.0, 0.0).astype(jnp.bfloat16)
    allowed = jnp.concatenate([allowed] * TOGETHER, axis=1)
    reach = jnp.zeros((1, rows), jnp.float32)
    for h in range(heads):
        turned = q_ref[0, :, head_columns(h)].T
        qt_ref[0, 0, :, h * rows : (h + 1) * rows] = turned
        turned = turned.astype(jnp.float32)
        reach = jnp.maximum(reach, jnp.sum(turned * turned, axis=0, keepdims=True))
    reach = jnp.broadcast_to(jnp.sqrt(jnp.max(reach)) * SCALE, reach_ref.shape[2:])
    near = in_range(reach, keys)
    reach_ref[0, 0] = jnp.where(near, reach, FAR)

    def scores(h, some):
        return times(keys, qt_ref[0, 0, :, h * rows : (h + some) * rows])

    @pl.when(near)
    def _():
        later = scores(0, TOGETHER)
        for h in range(0, heads, TOGETHER):
            s = later
            if h + TOGETHER < heads:
                later = scores(h + TOGETHER, TOGETHER)
            weights = jnp.exp2(s * SCALE).astype(jnp.bfloat16) * allowed
            state_ref[0, 0, :, h * rows : (h + TOGETHER) * rows] = times(values, weights)

    @pl.when(jnp.logical_not(near))
    def _():
        for h in range(heads):
            s = jnp.where(causal, scores(h, 1), NEVER)
            peak = jnp.max(s, axis=0, keepdims=True)
            weights = jnp.exp2((s - peak) * SCALE).astype(jnp.bfloat16)
            state_ref[0, 0, :, h * rows : (h + 1) * rows] = keep_shift(times(values, weights), peak)


def state_shapes(pairs, kv_heads, stacked):
    return [
        jax.ShapeDtypeStruct((pairs, kv_heads, HD, stacked), jnp.bfloat16),
        jax.ShapeDtypeStruct((pairs, kv_heads, 8, HD), jnp.float32),
        jax.ShapeDtypeStruct((pairs, kv_heads, HD + EXTRA_ROWS, stacked), jnp.float32),
    ]


def rubric_attention(first, some, query, key, value, state, after):
    pairs, rows, width = query.shape
    steps = key.shape[2] // HD
    step_width = width // steps
    stacked = step_width // HD * rows
    count = key.shape[1]

    def across(size):
        return pl.BlockSpec((1, rows, size), lambda p, g: (first + p, 0, g))

    return pl.pallas_call(
        rubric_kernel,
        grid=(some, steps),
        in_specs=[across(step_width), across(HD), across(HD)] + [ANY] * (1 + len(state)),
        out_specs=[
            pl.BlockSpec((1, 1, size, width), lambda p, g: (first + p, g, 0, 0))
            for size, width in ((HD, stacked), (8, HD), (HD + EXTRA_ROWS, stacked))
        ],
        out_shape=state_shapes(pairs, steps, stacked),
        input_output_aliases={4 + i: i for i in range(len(state))},
        compiler_params=params("arbitrary", "arbitrary"),
        cost_estimate=hint(
            6 * some * width * rows * count,
            some * rows * width * 8,
            some * width // HD * rows * count,
        ),
        name="rubric_attention",
    )(query, key, value, after, *state)


def response_kernel(shift, plan_ref, kv_ref, qt_ref, reach_ref, state_ref, *refs):
    reach_out, state_out, out_ref = refs[-3:]
    rows = out_ref.shape[1]
    heads = out_ref.shape[2] // HD
    count = kv_ref.shape[0] // 2
    length = plan_ref[shift * FIELDS + 2]
    wanted = plan_ref[shift * FIELDS + 3] == 1
    completes = plan_ref[shift * FIELDS + 4] == 1

    def stack(h, some):
        return slice(h * rows, (h + some) * rows)

    @pl.when(wanted)
    def _():
        keys = kv_ref[:count, :]
        values = turned_values(kv_ref[count:, :])
        live = lax.broadcasted_iota(jnp.int32, values.shape, 1) < length
        values = jnp.where(live, values, 0.0).astype(jnp.bfloat16)
        near = in_range(reach_ref[...], keys)

        def scores(h, some):
            return times(keys, qt_ref[0, 0, :, stack(h, some)])

        @pl.when(near)
        def _():
            reach_out[...] = reach_ref[...]
            later = scores(0, TOGETHER)
            for h in range(0, heads, TOGETHER):
                s = later
                if h + TOGETHER < heads:
                    later = scores(h + TOGETHER, TOGETHER)
                weights = jnp.exp2(s * SCALE).astype(jnp.bfloat16)
                at = stack(h, TOGETHER)
                state_out[0, 0, :, at] = state_ref[0, 0, :, at] + times(values, weights)

        @pl.when(jnp.logical_not(near))
        def _():
            reach_out[...] = jnp.full(reach_out.shape, FAR, jnp.float32)
            live_rows = lax.broadcasted_iota(jnp.int32, (count, rows), 0) < length
            for h in range(heads):
                s = jnp.where(live_rows, scores(h, 1), NEVER)
                old = state_ref[0, 0, :, stack(h, 1)]
                old_peak = old[SHIFT_ROW : SHIFT_ROW + 1]
                peak = jnp.maximum(old_peak, jnp.max(s, axis=0, keepdims=True))
                weights = jnp.exp2((s - peak) * SCALE).astype(jnp.bfloat16)
                new = old * jnp.exp2((old_peak - peak) * SCALE) + times(values, weights)
                state_out[0, 0, :, stack(h, 1)] = keep_shift(new, peak)

    @pl.when(jnp.logical_not(wanted))
    def _():
        reach_out[...] = reach_ref[...]
        state_out[...] = state_ref[...]

    @pl.when(completes | jnp.logical_not(wanted))
    def _():
        for h in range(heads):
            share = state_out[0, 0, :HD, stack(h, 1)] * (1.0 / state_out[0, 0, HD : HD + 1, stack(h, 1)])
            out_ref[0, :, head_columns(h)] = share.astype(out_ref.dtype).T


def response_attention(shift, plan, query, kv, state, out):
    pairs, rows, width = query.shape
    steps = kv.shape[1] // HD
    step_width = width // steps
    stacked = step_width // HD * rows
    count = kv.shape[0] // 2
    pair_at = shift * FIELDS + 1
    state_specs = [
        pl.BlockSpec((1, 1, size, columns), lambda g, plan: (plan[pair_at], g, 0, 0))
        for size, columns in ((HD, stacked), (8, HD), (HD + EXTRA_ROWS, stacked))
    ]
    operands = [plan, kv, *state]
    in_specs = [pl.BlockSpec((2 * count, HD), lambda g, plan: (0, g)), *state_specs]
    aliases = {3: 0, 4: 1}
    if out is not None:
        aliases[len(operands)] = 2
        operands.append(out)
        in_specs.append(ANY)
    results = pl.pallas_call(
        functools.partial(response_kernel, shift),
        grid_spec=pltpu.PrefetchScalarGridSpec(
            num_scalar_prefetch=1,
            grid=(steps,),
            in_specs=in_specs,
            out_specs=state_specs[1:]
            + [pl.BlockSpec((1, rows, step_width), lambda g, plan: (plan[pair_at], 0, g))],
        ),
        out_shape=state_shapes(pairs, steps, stacked)[1:]
        + [jax.ShapeDtypeStruct(query.shape, jnp.bfloat16)],
        input_output_aliases=aliases,
        compiler_params=params("arbitrary"),
        cost_estimate=hint(
            6 * width * rows * count, rows * width * 12, width // HD * rows * count
        ),
        name="response_attention",
    )(*operands)
    return [state[0], *results[:2]], results[2]


def local(
    rubric_query,
    rubric_key,
    rubric_value,
    response_states,
    key_weight,
    value_weight,
    owner_slot,
    response_length,
    pair_table,
):
    groups = lax.axis_size("dp")
    stored, length, depth = response_states.shape
    pairs = rubric_query.shape[0]
    tensor = lax.axis_size("tensor")
    width = key_weight.shape[1] // tensor
    me = lax.axis_index("dp").astype(jnp.int32)
    own_half = lax.axis_index("tensor").astype(jnp.int32)
    other_half = 1 - own_half
    rows = response_states.reshape(stored * length, depth)
    swap = [(0, 1), (1, 0)]
    order = arrival_order(groups)
    place = jnp.array([0] + [1 + order.index(s) for s in range(1, groups)], jnp.int32)
    tables = [owner_slot, response_length, pair_table.T, place]

    plan = make_plan(me, tables, groups, stored)
    def other_columns(part):
        return lax.dynamic_slice_in_dim(part, other_half * width, width, 1)

    own_keys = times(rows, key_weight)
    keys_in = lax.ppermute(other_columns(own_keys), "tensor", swap)
    own_values = times(rows, value_weight)
    values_in = lax.ppermute(other_columns(own_values), "tensor", swap)
    blocks = finish(
        plan, own_half, own_keys, own_values, keys_in, values_in, groups, length
    )
    arrived = {0: blocks[0]}

    def send(shifts, *after):
        for shift in shifts:
            block = lax.optimization_barrier((blocks[shift], *after))[0]
            arrived[shift] = lax.ppermute(block, "dp", [(g, g ^ shift) for g in range(groups)])

    send(order[:2])
    half = pairs // 2
    state = rubric_attention(
        0, half, rubric_query, rubric_key, rubric_value, (), blocks[0]
    )
    send(order[2:4], state[1])
    state = rubric_attention(
        half, pairs - half, rubric_query, rubric_key, rubric_value, state, arrived[order[1]]
    )
    state, out = response_attention(0, plan, rubric_query, blocks[0], state, None)
    for at in range(0, len(order), 2):
        send(order[at + 4 : at + 6], arrived[order[at]], state[1])
        for shift in order[at : at + 2]:
            state, out = response_attention(
                shift, plan, rubric_query, arrived[shift], state, out
            )
    return out


def solution(mesh):
    return jax.shard_map(
        local,
        mesh=mesh,
        in_specs=(
            P(("rep", "dp"), None, "tensor"),
            P(("rep", "dp"), None, "tensor"),
            P(("rep", "dp"), None, "tensor"),
            P(("rep", "dp"), None, "tensor"),
            P("tensor", None),
            P("tensor", None),
            P("rep"),
            P("rep"),
            P("rep", None),
        ),
        out_specs=P(("rep", "dp"), None, "tensor"),
        check_vma=False,
    )
```

```python
import functools
import math

import jax
import jax.numpy as jnp
from jax import lax
from jax.experimental import pallas as pl
from jax.experimental.pallas import tpu as pltpu
from jax.sharding import PartitionSpec as P

HD = 128
SCALE = HD ** (-0.5) * math.log2(math.e)
MIB = 1024 * 1024
FIELDS = 5
NEVER = -1e30
SUB_ROWS = 128
PART = 1
NEAR = 100.0
FAR = 1e30
TOGETHER = 2
EXTRA_ROWS = 16
SHIFT_ROW = HD + EXTRA_ROWS // 2
ANY = pl.BlockSpec(memory_space=pl.ANY)
SMEM = pl.BlockSpec(memory_space=pltpu.SMEM)
WHOLE = pl.BlockSpec(memory_space=pltpu.VMEM)


def params(*semantics, vmem=12):
    return pltpu.CompilerParams(
        dimension_semantics=semantics or None, vmem_limit_bytes=vmem * MIB
    )


def hint(flops, bytes_accessed, transcendentals, part=1):
    return pl.CostEstimate(
        flops=flops // part,
        bytes_accessed=bytes_accessed // part,
        transcendentals=transcendentals // part,
    )


def partners(groups):
    return list(range(groups - 1, groups // 2 - 1, -1)), list(range(groups // 2 - 1, 0, -1))


def order_of_use(groups):
    far, near = partners(groups)
    return [0] + near[:2] + far[:-1] + near[2:] + far[-1:]


def write_plan(groups, stored, me, owner_ref, length_ref, table_ref, place_ref, plan_ref):
    pairs = table_ref.shape[1] // groups
    bits = stored.bit_length() - 1

    def slot_of(group, j):
        response = table_ref[j % 2, group * pairs + j // 2]
        slot = owner_ref[response]
        return response, lax.shift_right_logical(slot, bits), slot & (stored - 1)

    for shift in range(groups):
        plan_ref[shift * FIELDS + 3] = 0
        plan_ref[shift * FIELDS + 1] = 0
        row = jnp.int32(0)
        for j in range(2 * pairs):
            _, source, slot_row = slot_of(me ^ shift, j)
            row = jnp.where(source == me, slot_row, row)
        plan_ref[shift * FIELDS] = row
    sources = [slot_of(me, j) for j in range(2 * pairs)]
    for j, (response, source, _) in enumerate(sources):
        shift = source ^ me
        later = place_ref[shift] > place_ref[sources[j ^ 1][1] ^ me]
        plan_ref[shift * FIELDS + 1] = jnp.int32(j // 2)
        plan_ref[shift * FIELDS + 2] = length_ref[response]
        plan_ref[shift * FIELDS + 3] = jnp.int32(1)
        plan_ref[shift * FIELDS + 4] = later.astype(jnp.int32)


def project_rows_kernel(groups, stored, half_ref, me_ref, owner_ref, length_ref, table_ref, place_ref, x_ref, key_ref, value_ref, out_ref, plan_ref):
    write_plan(groups, stored, me_ref[0], owner_ref, length_ref, table_ref, place_ref, plan_ref)
    width = key_ref.shape[1]
    for at in range(0, x_ref.shape[0], SUB_ROWS):
        part = slice(at, at + SUB_ROWS)
        out_ref[part, :width] = times(x_ref[part, :], key_ref[...])
        out_ref[part, width:] = times(x_ref[part, :], value_ref[...])


def project_and_plan(rows, key_weight, value_weight, half, width, me, tables, groups, stored):
    total, depth = rows.shape
    block = 256
    weight_spec = pl.BlockSpec((depth, width), lambda i, half, me: (0, half[0]))
    return pl.pallas_call(
        functools.partial(project_rows_kernel, groups, stored),
        grid_spec=pltpu.PrefetchScalarGridSpec(
            num_scalar_prefetch=2,
            grid=(total // block,),
            in_specs=[SMEM] * len(tables)
            + [pl.BlockSpec((block, depth), lambda i, half, me: (i, 0)), weight_spec, weight_spec],
            out_specs=[pl.BlockSpec((block, 2 * width), lambda i, half, me: (i, 0)), SMEM],
        ),
        out_shape=[
            jax.ShapeDtypeStruct((total, 2 * width), jnp.float32),
            jax.ShapeDtypeStruct((groups * FIELDS,), jnp.int32),
        ],
        compiler_params=params("arbitrary", vmem=60),
        cost_estimate=hint(
            4 * total * depth * width, 2 * total * depth + 4 * depth * width + 8 * total * width, 0
        ),
        name="other_half",
    )(half[None], me[None], *tables, rows, key_weight, value_weight)


def finish_kernel(length, width, plan_ref, own_keys_ref, own_values_ref, other_ref, *out_refs):
    for shift, out_ref in enumerate(out_refs):
        start = pl.multiple_of(plan_ref[shift * FIELDS] * length, length)
        rows = pl.ds(start, length)
        for at, own_ref in enumerate((own_keys_ref, own_values_ref)):
            total = own_ref[rows, :] + other_ref[rows, at * width : (at + 1) * width]
            out_ref[at * length : (at + 1) * length, :] = total.astype(out_ref.dtype)


def finish(plan, own_keys, own_values, other, groups, length, name):
    total, width = own_keys.shape
    return pl.pallas_call(
        functools.partial(finish_kernel, length, width),
        out_shape=[jax.ShapeDtypeStruct((2 * length, width), jnp.bfloat16)] * groups,
        in_specs=[SMEM, WHOLE, WHOLE, WHOLE],
        out_specs=[WHOLE] * groups,
        compiler_params=params(),
        cost_estimate=hint(
            2 * groups * length * width,
            16 * total * width + 4 * groups * length * width,
            0,
        ),
        name=name,
    )(plan, own_keys, own_values, other)


def times(a, b):
    return jnp.dot(a, b, preferred_element_type=jnp.float32)


def head_columns(h):
    return slice(h * HD, (h + 1) * HD)


def turned_values(values):
    count = values.shape[0]
    row = lax.broadcasted_iota(jnp.int32, (EXTRA_ROWS, count), 0)
    ones = jnp.where(row < EXTRA_ROWS // 2, 1.0, 0.0)
    return jnp.concatenate([values.astype(jnp.float32).T, ones], axis=0)


def longest_of(keys):
    keys = keys.astype(jnp.float32)
    return jnp.sqrt(jnp.max(jnp.sum(keys * keys, axis=1, keepdims=True)))


def in_range(reach, keys):
    return jnp.max(reach) * longest_of(keys) < NEAR


def keep_shift(state, shift):
    row = lax.broadcasted_iota(jnp.int32, state.shape, 0)
    return jnp.where(row >= SHIFT_ROW, shift, state)


def rubric_kernel(q_ref, k_ref, v_ref, *refs):
    qt_ref, reach_ref, state_ref = refs[-3:]
    rows = q_ref.shape[1]
    heads = q_ref.shape[2] // HD
    keys = k_ref[0]
    values = turned_values(v_ref[0]).astype(jnp.bfloat16)
    shape = (keys.shape[0], rows)
    causal = lax.broadcasted_iota(jnp.int32, shape, 0) <= lax.broadcasted_iota(jnp.int32, shape, 1)
    allowed = jnp.where(causal, 1.0, 0.0).astype(jnp.bfloat16)
    allowed = jnp.concatenate([allowed] * TOGETHER, axis=1)
    reach = jnp.zeros((1, rows), jnp.float32)
    for h in range(heads):
        turned = q_ref[0, :, head_columns(h)].T
        qt_ref[0, 0, :, h * rows : (h + 1) * rows] = turned
        turned = turned.astype(jnp.float32)
        reach = jnp.maximum(reach, jnp.sum(turned * turned, axis=0, keepdims=True))
    reach = jnp.broadcast_to(jnp.sqrt(jnp.max(reach)) * SCALE, reach_ref.shape[2:])
    near = in_range(reach, keys)
    reach_ref[0, 0] = jnp.where(near, reach, FAR)

    def scores(h, some):
        return times(keys, qt_ref[0, 0, :, h * rows : (h + some) * rows])

    @pl.when(near)
    def _():
        later = scores(0, TOGETHER)
        for h in range(0, heads, TOGETHER):
            s = later
            if h + TOGETHER < heads:
                later = scores(h + TOGETHER, TOGETHER)
            weights = jnp.exp2(s * SCALE).astype(jnp.bfloat16) * allowed
            state_ref[0, 0, :, h * rows : (h + TOGETHER) * rows] = times(values, weights)

    @pl.when(jnp.logical_not(near))
    def _():
        for h in range(heads):
            s = jnp.where(causal, scores(h, 1), NEVER)
            peak = jnp.max(s, axis=0, keepdims=True)
            weights = jnp.exp2((s - peak) * SCALE).astype(jnp.bfloat16)
            state_ref[0, 0, :, h * rows : (h + 1) * rows] = keep_shift(times(values, weights), peak)


def state_shapes(pairs, kv_heads, stacked):
    return [
        jax.ShapeDtypeStruct((pairs, kv_heads, HD, stacked), jnp.bfloat16),
        jax.ShapeDtypeStruct((pairs, kv_heads, 8, HD), jnp.float32),
        jax.ShapeDtypeStruct((pairs, kv_heads, HD + EXTRA_ROWS, stacked), jnp.float32),
    ]


def rubric_attention(first, some, query, key, value, state, after):
    pairs, rows, width = query.shape
    steps = key.shape[2] // HD
    step_width = width // steps
    stacked = step_width // HD * rows
    count = key.shape[1]

    def across(size):
        return pl.BlockSpec((1, rows, size), lambda p, g: (first + p, 0, g))

    return pl.pallas_call(
        rubric_kernel,
        grid=(some, steps),
        in_specs=[across(step_width), across(HD), across(HD)] + [ANY] * (1 + len(state)),
        out_specs=[
            pl.BlockSpec((1, 1, size, width), lambda p, g: (first + p, g, 0, 0))
            for size, width in ((HD, stacked), (8, HD), (HD + EXTRA_ROWS, stacked))
        ],
        out_shape=state_shapes(pairs, steps, stacked),
        input_output_aliases={4 + i: i for i in range(len(state))},
        compiler_params=params("arbitrary", "arbitrary"),
        cost_estimate=hint(
            6 * some * width * rows * count,
            some * rows * width * 8,
            some * width // HD * rows * count,
            part=PART,
        ),
        name="rubric_attention",
    )(query, key, value, after, *state)


def response_kernel(shift, plan_ref, kv_ref, qt_ref, reach_ref, state_ref, *refs):
    reach_out, state_out, out_ref = refs[-3:]
    rows = out_ref.shape[1]
    heads = out_ref.shape[2] // HD
    count = kv_ref.shape[0] // 2
    length = plan_ref[shift * FIELDS + 2]
    wanted = plan_ref[shift * FIELDS + 3] == 1
    completes = plan_ref[shift * FIELDS + 4] == 1

    def stack(h, some):
        return slice(h * rows, (h + some) * rows)

    @pl.when(wanted)
    def _():
        keys = kv_ref[:count, :]
        values = turned_values(kv_ref[count:, :])
        live = lax.broadcasted_iota(jnp.int32, values.shape, 1) < length
        values = jnp.where(live, values, 0.0).astype(jnp.bfloat16)
        near = in_range(reach_ref[...], keys)

        def scores(h, some):
            return times(keys, qt_ref[0, 0, :, stack(h, some)])

        @pl.when(near)
        def _():
            reach_out[...] = reach_ref[...]
            later = scores(0, TOGETHER)
            for h in range(0, heads, TOGETHER):
                s = later
                if h + TOGETHER < heads:
                    later = scores(h + TOGETHER, TOGETHER)
                weights = jnp.exp2(s * SCALE).astype(jnp.bfloat16)
                at = stack(h, TOGETHER)
                state_out[0, 0, :, at] = state_ref[0, 0, :, at] + times(values, weights)

        @pl.when(jnp.logical_not(near))
        def _():
            reach_out[...] = jnp.full(reach_out.shape, FAR, jnp.float32)
            live_rows = lax.broadcasted_iota(jnp.int32, (count, rows), 0) < length
            for h in range(heads):
                s = jnp.where(live_rows, scores(h, 1), NEVER)
                old = state_ref[0, 0, :, stack(h, 1)]
                old_peak = old[SHIFT_ROW : SHIFT_ROW + 1]
                peak = jnp.maximum(old_peak, jnp.max(s, axis=0, keepdims=True))
                weights = jnp.exp2((s - peak) * SCALE).astype(jnp.bfloat16)
                new = old * jnp.exp2((old_peak - peak) * SCALE) + times(values, weights)
                state_out[0, 0, :, stack(h, 1)] = keep_shift(new, peak)

    @pl.when(jnp.logical_not(wanted))
    def _():
        reach_out[...] = reach_ref[...]
        state_out[...] = state_ref[...]

    @pl.when(completes | jnp.logical_not(wanted))
    def _():
        for h in range(heads):
            share = state_out[0, 0, :HD, stack(h, 1)] * (1.0 / state_out[0, 0, HD : HD + 1, stack(h, 1)])
            out_ref[0, :, head_columns(h)] = share.astype(out_ref.dtype).T


def response_attention(shift, plan, query, kv, state, out):
    pairs, rows, width = query.shape
    steps = kv.shape[1] // HD
    step_width = width // steps
    stacked = step_width // HD * rows
    count = kv.shape[0] // 2
    pair_at = shift * FIELDS + 1
    state_specs = [
        pl.BlockSpec((1, 1, size, columns), lambda g, plan: (plan[pair_at], g, 0, 0))
        for size, columns in ((HD, stacked), (8, HD), (HD + EXTRA_ROWS, stacked))
    ]
    operands = [plan, kv, *state]
    in_specs = [pl.BlockSpec((2 * count, HD), lambda g, plan: (0, g)), *state_specs]
    aliases = {3: 0, 4: 1}
    if out is not None:
        aliases[len(operands)] = 2
        operands.append(out)
        in_specs.append(ANY)
    results = pl.pallas_call(
        functools.partial(response_kernel, shift),
        grid_spec=pltpu.PrefetchScalarGridSpec(
            num_scalar_prefetch=1,
            grid=(steps,),
            in_specs=in_specs,
            out_specs=state_specs[1:]
            + [pl.BlockSpec((1, rows, step_width), lambda g, plan: (plan[pair_at], 0, g))],
        ),
        out_shape=state_shapes(pairs, steps, stacked)[1:]
        + [jax.ShapeDtypeStruct(query.shape, jnp.bfloat16)],
        input_output_aliases=aliases,
        compiler_params=params("arbitrary"),
        cost_estimate=hint(
            6 * width * rows * count, rows * width * 12, width // HD * rows * count,
            part=PART,
        ),
        name="response_attention",
    )(*operands)
    return [state[0], *results[:2]], results[2]


def local(
    rubric_query,
    rubric_key,
    rubric_value,
    response_states,
    key_weight,
    value_weight,
    owner_slot,
    response_length,
    pair_table,
):
    groups = lax.axis_size("dp")
    stored, length, depth = response_states.shape
    pairs = rubric_query.shape[0]
    tensor = lax.axis_size("tensor")
    width = key_weight.shape[1] // tensor
    me = lax.axis_index("dp").astype(jnp.int32)
    own_half = lax.axis_index("tensor").astype(jnp.int32)
    other_half = 1 - own_half
    rows = response_states.reshape(stored * length, depth)
    swap = [(0, 1), (1, 0)]
    far, near = partners(groups)
    order = order_of_use(groups)
    place = jnp.array([order.index(shift) for shift in range(groups)], jnp.int32)
    tables = [owner_slot, response_length, pair_table.T, place]

    other, plan = project_and_plan(
        rows, key_weight, value_weight, other_half, width, me, tables, groups, stored
    )
    received = lax.ppermute(other, "tensor", swap)
    own_keys, own_values = (
        times(rows, lax.dynamic_slice_in_dim(weight, own_half * width, width, 1))
        for weight in (key_weight, value_weight)
    )
    blocks = finish(plan, own_keys, own_values, received, groups, length, "finish")
    arrived = {0: blocks[0]}

    def send(shifts, *after):
        for shift in shifts:
            block = lax.optimization_barrier((blocks[shift], *after))[0]
            arrived[shift] = lax.ppermute(block, "dp", [(g, g ^ shift) for g in range(groups)])

    send(far[:1] + near[:1])
    half = pairs // 2
    state = rubric_attention(0, half, rubric_query, rubric_key, rubric_value, (), blocks[0])
    send(far[1:2] + near[1:2], state[1])
    state = rubric_attention(
        half, pairs - half, rubric_query, rubric_key, rubric_value, state, blocks[0]
    )
    send(far[2:3], state[1], arrived[near[0]])
    to_send = [(shift, far[at]) for at, shift in enumerate(far[3:])]
    to_send += [(shift, far[at + 1]) for at, shift in enumerate(near[2:])]
    out = None
    for shift in order:
        while shift not in arrived:
            last, before = to_send.pop(0)
            send([last], state[1], arrived[before])
        state, out = response_attention(
            shift, plan, rubric_query, arrived[shift], state, out
        )
        for last, before in [entry for entry in to_send if entry[1] == shift]:
            to_send.remove((last, before))
            send([last], state[1], arrived[before])
    return out


def solution(mesh):
    return jax.shard_map(
        local,
        mesh=mesh,
        in_specs=(
            P(("rep", "dp"), None, "tensor"),
            P(("rep", "dp"), None, "tensor"),
            P(("rep", "dp"), None, "tensor"),
            P(("rep", "dp"), None, "tensor"),
            P("tensor", None),
            P("tensor", None),
            P("rep"),
            P("rep"),
            P("rep", None),
        ),
        out_specs=P(("rep", "dp"), None, "tensor"),
        check_vma=False,
    )
```
